256 devices in a mesh: tok: 4 (over z_hi), voc: 32 (over x, y, core), sub: 2 (over z_lo).
Axes of the slice: x: 4, y: 4, z: 8 (z_hi: 4, z_lo: 2; z = z_hi * 2 + z_lo), core: 2. Of those that a mesh axis runs over, the one named last changes fastest.
Arguments:
- final_state_vectors: bfloat16 [1024, 4096], P(('tok', 'sub')), may hold values from -40 to 40
- learner_output_weights: bfloat16 [4096, 81920], P(('tok', 'sub'), 'voc'), may hold values from -2 to 2
- mentor_raw_scores: bfloat16 [2048, 81920], P('tok', ('voc', 'sub')), may hold values from -256 to 256
- kept_source_lines: int32 [1024], P('tok'), may hold values from 0 to 2047, as said below
- group_sizes_list: int32 [32], replicated, may hold values from 1 to 64, 1024 in all
Outputs:
- head_grad: float32 [4096, 81920], P(('tok', 'sub'), 'voc')
- feature_grad: float32 [1024, 4096], P('voc', ('tok', 'sub'))
- logit_grad: bfloat16 [1024, 81920], P(('tok', 'sub'), 'voc')
- divergence: float32 [1024], P(('tok', 'sub'))
The draws below stay inside these ranges and needn't reach their ends.
Inputs may be any that keep to these rules, and one draw needn't show every extreme that they name: Rows b * 256 to (b + 1) * 256 - 1 of kept_source_lines are distinct, increasing, and lie in b * 512 to (b + 1) * 512 - 1, both ends included.
All inputs are finite; a program needn't handle non-finite values.
Results may differ from the reference program's by a relative error of at most 0.014.
Values may be sent and summed in bfloat16 or wider, within the bound.
No kernel may reach another device: no remote copies, remote signals or barrier semaphores. Data moves between devices by JAX's collectives and lax.ppermute only.
A program may use at most 128 MiB of HBM per device.

```python
import math
import jax
import jax.numpy as jnp
import numpy as np

D = 4096
SURV_TOK = 256
MEAN_LEN = 32
LOSS_SCALE = 65536
V = 81920
ROWS = 1024
POOL_TOK = 512
POOL = 2048
GROUPS = 32
N_TOK = 4


def draw_kept_source_lines(key, part):
    key = jax.random.fold_in(key, 11)
    block_keys = jax.random.split(key, N_TOK)

    def one_block(block_key, block_index):
        middle = jax.random.permutation(block_key, POOL_TOK - 2)[:SURV_TOK - 2].astype(jnp.int32) + 1
        chosen = jnp.concatenate([jnp.zeros((1,), jnp.int32), middle, jnp.full((1,), POOL_TOK - 1, jnp.int32)])
        return jnp.sort(chosen) + block_index * POOL_TOK
    picked = jax.vmap(one_block)(block_keys, jnp.arange(N_TOK, dtype=jnp.int32))
    return picked.reshape(-1).astype(jnp.int32)


def draw_final_state_vectors(key, part):
    key = jax.random.fold_in(key, 21)
    key_noise, key_rows = jax.random.split(key, 2)
    raw_noise = jnp.clip(jax.random.normal(key_noise, (ROWS, D), jnp.float32), -5.0, 5.0)
    row_scale = jnp.exp(jax.random.uniform(key_rows, (ROWS, 1), jnp.float32, math.log(0.02), math.log(0.2)))
    values = raw_noise * row_scale
    return jnp.clip(values, -40.0, 40.0).astype(jnp.bfloat16)


def draw_learner_output_weights(key, part):
    key = jax.random.fold_in(key, 31)
    key_noise, key_columns = jax.random.split(key, 2)
    column_ids = jnp.arange(V, dtype=jnp.int32)
    column_ramp = 1.0 + 0.3 * column_ids.astype(jnp.float32)[None, :] / V
    raw_noise = jnp.clip(jax.random.normal(key_noise, (D, V), jnp.float32), -5.0, 5.0)
    column_scale = jnp.exp(jax.random.uniform(key_columns, (1, V), jnp.float32, math.log(0.4), math.log(4.0)))
    values = raw_noise * column_scale * column_ramp / math.sqrt(D)
    return jnp.clip(values, -2.0, 2.0).astype(jnp.bfloat16)


def draw_mentor_raw_scores(key, part):
    key = jax.random.fold_in(key, 41)
    key_noise, key_rows, key_columns = jax.random.split(key, 3)
    column_ids = jnp.arange(V, dtype=jnp.int32)[None, :]
    vocab_rise = 1.1 * column_ids.astype(jnp.float32) / V
    raw_noise = jnp.clip(jax.random.normal(key_noise, (POOL, V), jnp.float32), -6.0, 6.0)
    row_scale = jnp.exp(jax.random.uniform(key_rows, (POOL, 1), jnp.float32, math.log(0.02), math.log(0.2)))
    column_scale = jnp.exp(jax.random.uniform(key_columns, (1, V), jnp.float32, math.log(0.4), math.log(4.0)))
    values = raw_noise * row_scale * column_scale + vocab_rise
    return jnp.clip(values, -256.0, 256.0).astype(jnp.bfloat16)


def split_up(count, total, most, slope):
    weights = [(1 << 20) // math.isqrt(rank ** slope) + 1 for rank in range(2, count + 1)]
    rest, given = total - most - (count - 1), [1] * (count - 1)
    while rest > 0:
        candidates = [i for i in range(count - 1) if given[i] < most]
        whole, budget = sum([weights[i] for i in candidates]), rest
        for i in candidates:
            extra = min(most - given[i], max(1, budget * weights[i] // whole), rest)
            given[i] = given[i] + extra
            rest = rest - extra
    return np.array([most] + given)


def ragged_sizes(stream_key, number_of, total, limit, lean):
    if number_of == 2:
        one = jax.random.randint(stream_key, (), max(1, total - limit), min(limit, total - 1) + 1)
        return jnp.stack([one, total - one])
    tallies = jnp.asarray(split_up(number_of, total, limit, lean), jnp.int32)
    pairs = (number_of - 1) // 2
    donor, sink = tallies[1:1 + 2 * pairs:2], tallies[2:2 + 2 * pairs:2]
    margin = jnp.minimum(donor - 1, limit - sink)
    passed = jax.random.randint(jax.random.fold_in(stream_key, 1), (pairs,), 0, 1 << 20) % (margin + 1)
    tallies = tallies.at[1:1 + 2 * pairs:2].set(donor - passed).at[2:2 + 2 * pairs:2].set(sink + passed)
    return tallies[jax.random.permutation(jax.random.fold_in(stream_key, 2), number_of)]


def setup_inputs(seed: int = 0) -> dict:
    key_of = jax.random.split(jax.random.key(seed), 6)
    final_state_vectors = draw_final_state_vectors(jax.random.fold_in(key_of[5], 71), 0)
    learner_output_weights = draw_learner_output_weights(jax.random.fold_in(key_of[5], 71), 0)
    mentor_raw_scores = draw_mentor_raw_scores(jax.random.fold_in(key_of[5], 71), 0)
    kept_source_lines = draw_kept_source_lines(jax.random.fold_in(key_of[5], 71), 0)
    group_sizes_list = ragged_sizes(key_of[4], GROUPS, ROWS, 2 * MEAN_LEN, 1).astype(jnp.int32)
    return {"final_state_vectors": final_state_vectors, "learner_output_weights": learner_output_weights, "mentor_raw_scores": mentor_raw_scores, "kept_source_lines": kept_source_lines, "group_sizes_list": group_sizes_list}


def group_weights(group_sizes_list, row_ids):
    ends = jnp.cumsum(group_sizes_list).astype(jnp.int32)
    starts = ends - group_sizes_list
    member = (row_ids[:, None] >= starts[None, :]) & (row_ids[:, None] < ends[None, :])
    length_of = jnp.sum(jnp.where(member, group_sizes_list[None, :], 0), axis=1).astype(jnp.float32)
    return jnp.float32(LOSS_SCALE) / (jnp.float32(group_sizes_list.shape[0]) * length_of)


def reference(final_state_vectors, learner_output_weights, mentor_raw_scores, kept_source_lines, group_sizes_list):
    student = jnp.dot(final_state_vectors, learner_output_weights, preferred_element_type=jnp.float32)
    mentor_network = jnp.take(mentor_raw_scores, kept_source_lines, axis=0).astype(jnp.float32)
    student_top = jnp.max(student, axis=1, keepdims=True)
    learner_exponential = jnp.exp(student - student_top)
    student_total = jnp.sum(learner_exponential, axis=1, keepdims=True)
    teacher_top = jnp.max(mentor_network, axis=1, keepdims=True)
    mentor_exponential = jnp.exp(mentor_network - teacher_top)
    teacher_total = jnp.sum(mentor_exponential, axis=1, keepdims=True)
    cross_total = jnp.sum(mentor_exponential * (mentor_network - student), axis=1, keepdims=True)
    divergence = cross_total / teacher_total - teacher_top - jnp.log(teacher_total) + student_top + jnp.log(student_total)
    weights = group_weights(group_sizes_list, jnp.arange(ROWS, dtype=jnp.int32))
    logit_grad = (weights[:, None] * (learner_exponential / student_total - mentor_exponential / teacher_total)).astype(jnp.bfloat16)
    head_grad = jnp.dot(final_state_vectors.T, logit_grad, preferred_element_type=jnp.float32)
    feature_grad = jnp.dot(logit_grad, learner_output_weights.T, preferred_element_type=jnp.float32)
    return head_grad, feature_grad, logit_grad, divergence[:, 0]
```

```python
import jax
import jax.numpy as jnp
from jax import lax
from jax.experimental import pallas as pl
from jax.experimental.pallas import tpu as pltpu
from jax.sharding import PartitionSpec as P

LOSS_SCALE = 65536
F32 = jnp.float32
BF16 = jnp.bfloat16
RING = ("tok", "sub")


def row_weights(sizes, rows):
    count = sizes.shape[0]
    upto = lax.broadcasted_iota(jnp.int32, (count, count), 0) <= lax.broadcasted_iota(
        jnp.int32, (count, count), 1
    )
    ends = jnp.sum(jnp.where(upto, sizes[:, None], 0), axis=0)
    starts = ends - sizes
    ids = lax.broadcasted_iota(jnp.int32, (count, rows), 1)
    member = (ids >= starts[:, None]) & (ids < ends[:, None])
    lengths = jnp.sum(jnp.where(member, sizes[:, None], 0), axis=0).astype(F32)
    return F32(LOSS_SCALE) / (F32(count) * lengths)


def student_kernel(head_ref, rows_ref, student_ref, lse_ref):
    step = pl.program_id(0)
    part = jnp.dot(head_ref[0], rows_ref[...], preferred_element_type=F32)

    @pl.when(step == 0)
    def _():
        student_ref[...] = part

    @pl.when(step > 0)
    def _():
        student_ref[...] += part

    @pl.when(step == pl.num_programs(0) - 1)
    def _():
        logits = student_ref[...]
        top = jnp.max(logits, axis=0, keepdims=True)
        lse_ref[...] = top + jnp.log(jnp.sum(jnp.exp(logits - top), axis=0, keepdims=True))


def student_logits(head, rows):
    blocks, v, d = head.shape
    r = rows.shape[1]
    return pl.pallas_call(
        student_kernel,
        grid=(blocks,),
        in_specs=[
            pl.BlockSpec((1, v, d), lambda i: (i, 0, 0)),
            pl.BlockSpec((d, r), lambda i: (i, 0)),
        ],
        out_specs=[
            pl.BlockSpec((v, r), lambda i: (0, 0)),
            pl.BlockSpec((1, r), lambda i: (0, 0)),
        ],
        out_shape=[
            jax.ShapeDtypeStruct((v, r), F32),
            jax.ShapeDtypeStruct((1, r), F32),
        ],
        compiler_params=pltpu.CompilerParams(vmem_limit_bytes=32 * 1024 * 1024),
    )(head, rows)


def grad_kernel(student_ref, teacher_ref, scale_ref, grad_ref, cross_ref):
    student = student_ref[...]
    teacher = teacher_ref[0].astype(F32)
    chance = jnp.exp(teacher - scale_ref[1:2, :])
    cross_ref[...] = jnp.sum(chance * (teacher - student), axis=0, keepdims=True)
    grad = scale_ref[2:3, :] * (jnp.exp(student - scale_ref[0:1, :]) - chance)
    grad_ref[...] = grad.astype(BF16)


def logit_grads(student, teacher, scales):
    v, r = student.shape
    parts, _, width = teacher.shape
    return pl.pallas_call(
        grad_kernel,
        grid=(parts,),
        in_specs=[
            pl.BlockSpec((v, width), lambda i: (0, i)),
            pl.BlockSpec((1, v, width), lambda i: (i, 0, 0)),
            pl.BlockSpec((3, width), lambda i: (0, i)),
        ],
        out_specs=[
            pl.BlockSpec((v, width), lambda i: (0, i)),
            pl.BlockSpec((1, width), lambda i: (0, i)),
        ],
        out_shape=[
            jax.ShapeDtypeStruct((v, r), BF16),
            jax.ShapeDtypeStruct((1, r), F32),
        ],
        compiler_params=pltpu.CompilerParams(vmem_limit_bytes=32 * 1024 * 1024),
    )(student, teacher, scales)


def to_all(values, axis):
    size = lax.axis_size(axis)
    return lax.all_to_all(jnp.broadcast_to(values[None], (size,) + values.shape), axis, 0, 0)


def merge(parts):
    top = jnp.max(parts, axis=0)
    return top + jnp.log(jnp.sum(jnp.exp(parts - top[None]), axis=0))


def on_device(hidden, head, pool, lines, sizes):
    toks, subs, vocs = lax.axis_size("tok"), lax.axis_size("sub"), lax.axis_size("voc")
    ring = toks * subs
    share, width = hidden.shape
    rows = share * ring
    depth, vocab = head.shape
    cut = vocab // ring
    place = lax.axis_index(RING)
    core = lax.axis_index("voc") % 2

    piece = width // vocs
    own = lax.dynamic_slice_in_dim(hidden, lax.axis_index("voc") * piece, piece, 1)
    column = to_all(own, RING).reshape(rows, piece).T
    features = lax.all_gather(column, "voc", axis=0, tiled=True)

    slices = head.reshape(depth, subs, toks, cut).transpose(2, 1, 3, 0).reshape(ring, cut, depth)
    head_cut = lax.all_to_all(slices, RING, 0, 0)

    wanted = lines - lax.axis_index("tok") * pool.shape[0]
    choose = (
        lax.broadcasted_iota(jnp.int32, (pool.shape[0], lines.shape[0]), 0) == wanted[None, :]
    ).astype(BF16)
    picked = lax.dot_general(
        pool, choose, (((0,), (0,)), ((), ())), preferred_element_type=F32
    ).astype(BF16)
    teacher = lax.all_to_all(picked.reshape(toks, cut, lines.shape[0]), "tok", 0, 0)

    student, student_lse = student_logits(head_cut, features)
    teacher_wide = teacher.astype(F32)
    teacher_top = jnp.max(teacher_wide, axis=1)
    teacher_lse = teacher_top + jnp.log(
        jnp.sum(jnp.exp(teacher_wide - teacher_top[:, None]), axis=1)
    )
    stats = jnp.stack([student_lse.reshape(8, rows // 8), teacher_lse.reshape(8, rows // 8)])
    stats = merge(to_all(stats, RING))
    stats = merge(to_all(stats, "voc")).reshape(2, rows)

    weights = row_weights(sizes, rows)
    scales = jnp.concatenate([stats, weights[None]])
    grad_cut, cross = logit_grads(student, teacher, scales)
    grads = lax.all_gather(grad_cut, ("sub", "tok"), axis=0, tiled=True)

    cross = jnp.sum(lax.all_to_all(cross.reshape(ring, share), RING, 0, 0), axis=0)
    cross = jnp.sum(to_all(cross, "voc"), axis=0)
    own_stats = lax.dynamic_slice_in_dim(stats, place * share, share, 1)
    divergence = cross + own_stats[0] - own_stats[1]

    feature_part = lax.dot_general(
        grads, head, (((0,), (1,)), ((), ())), preferred_element_type=F32
    )
    chips = vocs // 2
    halves = feature_part.reshape(chips, 2, rows // vocs, depth)
    keep = jnp.where(core == 0, halves[:, 0], halves[:, 1])
    give = jnp.where(core == 0, halves[:, 1], halves[:, 0])
    given = lax.ppermute(give, "voc", [(i, i ^ 1) for i in range(vocs)])
    groups = [[2 * i + c for i in range(chips)] for c in range(2)]
    sums = lax.all_to_all((keep + given).astype(BF16), "voc", 0, 0, axis_index_groups=groups)
    feature_grad = jnp.sum(sums.astype(F32), axis=0)

    own_features = lax.dynamic_slice_in_dim(features, place * depth, depth, 0)
    head_grad = lax.dot_general(
        own_features, grads, (((1,), (1,)), ((), ())), preferred_element_type=F32
    )
    local_grad = lax.dynamic_slice_in_dim(grads, place * share, share, 1).T
    return head_grad, feature_grad, local_grad, divergence


def solution(mesh):
    return jax.shard_map(
        on_device,
        mesh=mesh,
        in_specs=(
            P(RING, None),
            P(RING, "voc"),
            P("tok", ("voc", "sub")),
            P("tok"),
            P(),
        ),
        out_specs=(
            P(RING, "voc"),
            P("voc", RING),
            P(RING, "voc"),
            P(RING),
        ),
        check_vma=False,
    )
```

```python
import functools

import jax
import jax.numpy as jnp
from jax import lax
from jax.experimental import pallas as pl
from jax.experimental.pallas import tpu as pltpu
from jax.sharding import PartitionSpec as P

LOSS_SCALE = 65536
F32 = jnp.float32
BF16 = jnp.bfloat16
RING = ("tok", "sub")


def row_weights(sizes, rows):
    count = sizes.shape[0]
    upto = lax.broadcasted_iota(jnp.int32, (count, count), 0) <= lax.broadcasted_iota(
        jnp.int32, (count, count), 1
    )
    ends = jnp.sum(jnp.where(upto, sizes[:, None], 0), axis=0)
    starts = ends - sizes
    ids = lax.broadcasted_iota(jnp.int32, (count, rows), 1)
    member = (ids >= starts[:, None]) & (ids < ends[:, None])
    lengths = jnp.sum(jnp.where(member, sizes[:, None], 0), axis=0).astype(F32)
    return F32(LOSS_SCALE) / (F32(count) * lengths)


def student_kernel(head_ref, rows_ref, student_ref, lse_ref):
    step = pl.program_id(0)
    part = jnp.dot(head_ref[0], rows_ref[...], preferred_element_type=F32)

    @pl.when(step == 0)
    def _():
        student_ref[...] = part

    @pl.when(step > 0)
    def _():
        student_ref[...] += part

    @pl.when(step == pl.num_programs(0) - 1)
    def _():
        logits = student_ref[...]
        top = jnp.max(logits, axis=0, keepdims=True)
        lse_ref[...] = top + jnp.log(jnp.sum(jnp.exp(logits - top), axis=0, keepdims=True))


def student_logits(head, rows, subs):
    blocks, v, d = head.shape
    r = rows.shape[1]
    toks = blocks // subs
    return pl.pallas_call(
        student_kernel,
        grid=(blocks,),
        in_specs=[
            pl.BlockSpec((1, v, d), lambda i: (i, 0, 0)),
            pl.BlockSpec((d, r), lambda i: (i % toks * subs + i // toks, 0)),
        ],
        out_specs=[
            pl.BlockSpec((v, r), lambda i: (0, 0)),
            pl.BlockSpec((1, r), lambda i: (0, 0)),
        ],
        out_shape=[
            jax.ShapeDtypeStruct((v, r), F32),
            jax.ShapeDtypeStruct((1, r), F32),
        ],
        compiler_params=pltpu.CompilerParams(vmem_limit_bytes=58 * 1024 * 1024),
    )(head, rows)


def grad_kernel(tok_ref, student_ref, *refs):
    teacher_refs, (scale_ref, low_ref, high_ref, cross_ref) = refs[:-4], refs[-4:]
    toks = len(teacher_refs)
    width = teacher_refs[0].shape[1]
    half = low_ref.shape[0]
    for shift, teacher_ref in enumerate(teacher_refs):
        block = lax.rem(tok_ref[0] + toks - shift, toks)
        cols = pl.ds(pl.multiple_of(block * width, width), width)
        student = student_ref[:, cols]
        teacher = teacher_ref[...].astype(F32)
        chance = jnp.exp(teacher - scale_ref[1:2, cols])
        cross_ref[:, cols] = jnp.sum(chance * (teacher - student), axis=0, keepdims=True)
        grad = scale_ref[2:3, cols] * (jnp.exp(student - scale_ref[0:1, cols]) - chance)
        grad = grad.astype(BF16)
        low_ref[:, cols] = grad[:half]
        high_ref[:, cols] = grad[half:]


def logit_grads(tok, student, teachers, scales):
    v, r = student.shape
    vmem = pl.BlockSpec(memory_space=pltpu.VMEM)
    return pl.pallas_call(
        grad_kernel,
        in_specs=[pl.BlockSpec(memory_space=pltpu.SMEM)] + [vmem] * (2 + len(teachers)),
        out_specs=[vmem] * 3,
        out_shape=[
            jax.ShapeDtypeStruct((v // 2, r), BF16),
            jax.ShapeDtypeStruct((v // 2, r), BF16),
            jax.ShapeDtypeStruct((1, r), F32),
        ],
        compiler_params=pltpu.CompilerParams(vmem_limit_bytes=32 * 1024 * 1024),
    )(tok, student, *teachers, scales)


def fetch_blocks(where_ref, block_refs, hops, all_ref, sem):
    height = block_refs[0].shape[0]
    ring = all_ref.shape[0] // (2 * height)
    copies = []
    for index, (block_ref, (back, half)) in enumerate(zip(block_refs, hops)):
        origin = lax.rem(where_ref[0] + ring - back, ring)
        slot = lax.rem(origin, 2) * (ring // 2) + origin // 2
        start = pl.multiple_of(slot * (2 * height) + half * height, 16)
        copies.append(
            pltpu.make_async_copy(block_ref, all_ref.at[pl.ds(start, height)], sem.at[index])
        )
    for copy in copies:
        copy.start()
    for copy in copies:
        copy.wait()


def feature_kernel(hops, where_ref, *refs):
    blocks, (head_ref, keep_ref, give_ref, all_ref, sem) = refs[: len(hops)], refs[len(hops) :]
    fetch_blocks(where_ref, blocks, hops, all_ref, sem)
    first = where_ref[1] == 0
    tile = 256
    per = keep_ref.shape[1]
    chips = tile // (2 * per)

    @pl.loop(0, all_ref.shape[1] // tile)
    def _(i):
        cols = pl.ds(pl.multiple_of(i * tile, tile), tile)
        part = jnp.dot(head_ref[...], all_ref[:, cols], preferred_element_type=F32).T
        part = part.reshape(chips, 2, per, part.shape[1])
        even, odd = part[:, 0], part[:, 1]
        keep_ref[pl.ds(i * chips, chips)] = jnp.where(first, even, odd)
        give_ref[pl.ds(i * chips, chips)] = jnp.where(first, odd, even)


def feature_parts(where, blocks, hops, head, per):
    depth, vocab = head.shape
    rows = blocks[0].shape[1]
    vmem = pl.BlockSpec(memory_space=pltpu.VMEM)
    shape = jax.ShapeDtypeStruct((rows // (2 * per), per, depth), F32)
    return pl.pallas_call(
        functools.partial(feature_kernel, hops),
        in_specs=[pl.BlockSpec(memory_space=pltpu.SMEM)]
        + [pl.BlockSpec(memory_space=pl.ANY)] * len(blocks)
        + [vmem],
        out_specs=[vmem] * 2,
        out_shape=[shape, shape],
        scratch_shapes=[pltpu.VMEM((vocab, rows), BF16), pltpu.SemaphoreType.DMA((len(blocks),))],
        compiler_params=pltpu.CompilerParams(vmem_limit_bytes=40 * 1024 * 1024),
        cost_estimate=pl.CostEstimate(
            flops=2 * rows * depth * vocab, bytes_accessed=12 * 1024 * 1024, transcendentals=0
        ),
    )(where, *blocks, head)


def head_kernel(hops, where_ref, *refs):
    blocks, rest = refs[: len(hops)], refs[len(hops) :]
    features_ref, out_ref, own_ref, all_ref, own_features, sem, other_sem = rest
    depth = own_features.shape[0]
    mine = pl.ds(pl.multiple_of(where_ref[0] * depth, depth), depth)
    copy = pltpu.make_async_copy(features_ref.at[mine], own_features, other_sem)
    copy.start()
    fetch_blocks(where_ref, blocks, hops, all_ref, sem)
    copy.wait()
    tile = 256
    share = own_ref.shape[0]
    own_cols = pl.ds(pl.multiple_of(where_ref[0] * share, share), share)

    @pl.loop(0, all_ref.shape[0] // tile)
    def _(i):
        rows = pl.ds(pl.multiple_of(i * tile, tile), tile)
        out_ref[:, rows] = lax.dot_general(
            own_features[...],
            all_ref[rows, :],
            (((1,), (1,)), ((), ())),
            preferred_element_type=F32,
        )
        own_ref[:, rows] = all_ref[rows, own_cols].astype(F32).T.astype(BF16)


def head_parts(where, blocks, hops, features, depth, vocab, share):
    rows = blocks[0].shape[1]
    vmem = pl.BlockSpec(memory_space=pltpu.VMEM)
    return pl.pallas_call(
        functools.partial(head_kernel, hops),
        in_specs=[pl.BlockSpec(memory_space=pltpu.SMEM)]
        + [pl.BlockSpec(memory_space=pl.ANY)] * (len(blocks) + 1),
        out_specs=[vmem] * 2,
        out_shape=[
            jax.ShapeDtypeStruct((depth, vocab), F32),
            jax.ShapeDtypeStruct((share, vocab), BF16),
        ],
        scratch_shapes=[
            pltpu.VMEM((vocab, rows), BF16),
            pltpu.VMEM((depth, rows), BF16),
            pltpu.SemaphoreType.DMA((len(blocks),)),
            pltpu.SemaphoreType.DMA,
        ],
        compiler_params=pltpu.CompilerParams(vmem_limit_bytes=58 * 1024 * 1024),
        cost_estimate=pl.CostEstimate(
            flops=2 * rows * depth * vocab, bytes_accessed=12 * 1024 * 1024, transcendentals=0
        ),
    )(where, *blocks, features)


def to_all(values, axis, **groups):
    size = lax.axis_size(axis)
    if groups:
        size = len(groups["axis_index_groups"][0])
    return lax.all_to_all(jnp.broadcast_to(values[None], (size,) + values.shape), axis, 0, 0, **groups)


def merge(parts, axis=0):
    top = jnp.max(parts, axis=axis, keepdims=True)
    total = jnp.sum(jnp.exp(parts - top), axis=axis, keepdims=True)
    return jnp.squeeze(top + jnp.log(total), axis)


def ring_shift(values, step, size):
    return lax.ppermute(values, RING, [(i, (i + step) % size) for i in range(size)])


def ring_gather(halves, size):
    blocks, hops = list(halves), [(0, 0), (0, 1)]
    ahead, behind = list(halves), list(halves)
    for step in range(1, size // 2 + 1):
        last = step == size // 2
        for half in range(2):
            if not last or half == 1:
                ahead[half] = ring_shift(ahead[half], 1, size)
                blocks.append(ahead[half])
                hops.append((step, half))
            if not last or half == 0:
                behind[half] = ring_shift(behind[half], -1, size)
                blocks.append(behind[half])
                hops.append((size - step, half))
    return blocks, hops


def on_device(hidden, head, pool, lines, sizes):
    toks, subs, vocs = lax.axis_size("tok"), lax.axis_size("sub"), lax.axis_size("voc")
    ring = toks * subs
    chips = vocs // 2
    share, width = hidden.shape
    rows = share * ring
    depth, vocab = head.shape
    cut = vocab // ring
    kept = lines.shape[0]
    tok = lax.axis_index("tok")
    place = lax.axis_index(RING)
    core = lax.axis_index("voc") % 2
    cores = [(i, i ^ 1) for i in range(vocs)]
    groups = [[2 * i + c for i in range(chips)] for c in range(2)]

    wanted = lines - tok * pool.shape[0]
    choose = (
        lax.broadcasted_iota(jnp.int32, (pool.shape[0], kept), 0) == wanted[None, :]
    ).astype(BF16)
    picked = lax.dot_general(
        pool, choose, (((0,), (0,)), ((), ())), preferred_element_type=F32
    )
    teacher_lse = merge(picked).reshape(kept // 128, 128)
    picked = picked.astype(BF16).reshape(toks, cut, kept)

    piece = width // vocs
    own = lax.dynamic_slice_in_dim(hidden, lax.axis_index("voc") * piece, piece, 1)
    column = to_all(own, RING)
    slices = head.T.reshape(ring, cut, depth)
    slices, picked, teacher_lse, column = lax.optimization_barrier(
        (slices, picked, teacher_lse, column)
    )
    features = lax.all_gather(column.reshape(rows, piece).T, "voc", axis=0, tiled=True)
    head_cut = lax.all_to_all(slices, ("sub", "tok"), 0, 0)
    head_cut, picked = lax.optimization_barrier((head_cut, picked))

    teachers = []
    for shift in range(toks):
        part = lax.dynamic_index_in_dim(picked, (tok + shift) % toks, 0, keepdims=False)
        if shift:
            part = lax.ppermute(part, "tok", [(i, (i + shift) % toks) for i in range(toks)])
        teachers.append(part)

    student, student_lse = student_logits(head_cut, features, subs)
    stats = jnp.concatenate([student_lse.reshape(rows // 128, 128), teacher_lse])
    stats = to_all(stats, RING)
    ours = merge(stats[:, : rows // 128])
    theirs = stats[:, rows // 128 :].reshape(toks, subs, kept // 128, 128)
    stats = jnp.stack([ours, merge(theirs, 1).reshape(rows // 128, 128)])
    stats = merge(jnp.stack([stats, lax.ppermute(stats, "voc", cores)]))
    stats = merge(to_all(stats, "voc", axis_index_groups=groups)).reshape(2, rows)

    scales = jnp.concatenate([stats, row_weights(sizes, rows)[None]])
    low, high, cross = logit_grads(tok.reshape(1), student, teachers, scales)
    blocks, hops = ring_gather((low, high), ring)

    cross = jnp.sum(lax.all_to_all(cross.reshape(ring, share), RING, 0, 0), axis=0)
    cross = jnp.sum(to_all(cross, "voc"), axis=0)
    own_stats = lax.dynamic_slice_in_dim(stats, place * share, share, 1)
    divergence = cross + own_stats[0] - own_stats[1]
    *blocks, divergence = lax.optimization_barrier((*blocks, divergence))

    where = jnp.stack([place, core])
    keep, give = feature_parts(where, blocks, hops, head, rows // vocs)
    given = lax.ppermute(give, "voc", cores)
    sums, where = lax.optimization_barrier(((keep + given).astype(BF16), where))
    sums = lax.all_to_all(sums, "voc", 0, 0, axis_index_groups=groups)
    feature_grad = jnp.sum(sums.astype(F32), axis=0)

    head_grad, local_grad = head_parts(where, blocks, hops, features, depth, vocab, share)
    return head_grad, feature_grad, local_grad, divergence


def solution(mesh):
    return jax.shard_map(
        on_device,
        mesh=mesh,
        in_specs=(
            P(RING, None),
            P(RING, "voc"),
            P("tok", ("voc", "sub")),
            P("tok"),
            P(),
        ),
        out_specs=(
            P(RING, "voc"),
            P("voc", RING),
            P(RING, "voc"),
            P(RING),
        ),
        check_vma=False,
    )
```

```python
import functools
import math

import jax
import jax.numpy as jnp
from jax import lax
from jax.experimental import pallas as pl
from jax.experimental.pallas import tpu as pltpu
from jax.sharding import PartitionSpec as P

LOSS_SCALE = 65536
F32 = jnp.float32
BF16 = jnp.bfloat16
RING = ("tok", "sub")


def row_weights(sizes, rows):
    count = sizes.shape[0]
    upto = lax.broadcasted_iota(jnp.int32, (count, count), 0) <= lax.broadcasted_iota(
        jnp.int32, (count, count), 1
    )
    ends = jnp.sum(jnp.where(upto, sizes[:, None], 0), axis=0)
    starts = ends - sizes
    ids = lax.broadcasted_iota(jnp.int32, (count, rows), 1)
    member = (ids >= starts[:, None]) & (ids < ends[:, None])
    lengths = jnp.sum(jnp.where(member, sizes[:, None], 0), axis=0).astype(F32)
    return F32(LOSS_SCALE) / (F32(count) * lengths)


MIB = 1024 * 1024
VMEM = pl.BlockSpec(memory_space=pltpu.VMEM)
SMEM = pl.BlockSpec(memory_space=pltpu.SMEM)
HBM = pl.BlockSpec(memory_space=pl.ANY)


def params(mib):
    return pltpu.CompilerParams(vmem_limit_bytes=mib * MIB)


def log_sum_exp(values):
    top = jnp.max(values, axis=0, keepdims=True)
    return top + jnp.log(jnp.sum(jnp.exp(values - top), axis=0, keepdims=True))


def merged(stats):
    k = stats.shape[1] // 3
    student, teacher, cross = stats[:, :k], stats[:, k : 2 * k], stats[:, 2 * k :]
    student_lse, teacher_lse = log_sum_exp(student), log_sum_exp(teacher)
    cross = jnp.sum(jnp.exp(teacher - teacher_lse) * cross, axis=0)
    return student_lse[0], teacher_lse[0], cross


def place_columns(voc, side, array_refs, origins, out_ref, sem):
    core, chip = lax.rem(voc, 2), voc // 2
    x, y = chip // side, lax.rem(chip, side)
    copies = []
    for array_ref, (steps, other, which) in zip(array_refs, origins):
        half = array_ref.shape[0] // len(steps)
        for index, (back_x, back_y) in enumerate(steps):
            from_x = lax.rem(x + side - back_x, side)
            from_y = lax.rem(y + side - back_y, side)
            from_core = 1 - core if other else core
            start = ((from_x * side + from_y) * 2 + from_core) * (2 * half) + which * half
            copy = pltpu.make_async_copy(
                array_ref.at[index * half : (index + 1) * half],
                out_ref.at[pl.ds(pl.multiple_of(start, half), half)],
                sem.at[len(copies)],
            )
            copy.start()
            copies.append(copy)
    return copies


def student_kernel(order, side, origins, where_ref, head_ref, teacher_ref, *refs):
    arrays, rest = refs[: len(origins)], refs[len(origins) :]
    student_ref, stats_ref, own_ref, features, sem = rest
    depth = head_ref.shape[2]
    for copy in place_columns(where_ref[2], side, arrays, origins, features, sem):
        copy.wait()
    mine = pl.multiple_of(where_ref[0] * depth, depth)
    own_ref[...] = features[pl.ds(mine, depth), :]
    copies, height, lanes = stats_ref.shape
    toks, _, width = teacher_ref.shape

    @pl.loop(0, toks)
    def _(i):
        cols = pl.ds(pl.multiple_of(i * width, width), width)
        student = None
        for index, block in enumerate(order):
            part = jnp.dot(
                head_ref[index],
                features[block * depth : (block + 1) * depth, cols],
                preferred_element_type=F32,
            )
            student = part if student is None else student + part
        student_ref[:, cols] = student
        teacher = teacher_ref[i].astype(F32)
        student_lse, teacher_lse = log_sum_exp(student), log_sum_exp(teacher)
        cross = jnp.sum(
            jnp.exp(teacher - teacher_lse) * (teacher - student), axis=0, keepdims=True
        )
        pieces = width // lanes
        for index, row in enumerate((student_lse, teacher_lse, cross)):
            for piece in range(pieces):
                place = index * (height // 3) + i * pieces + piece
                values = row[:, piece * lanes : (piece + 1) * lanes]
                stats_ref[:, pl.ds(place, 1), :] = jnp.broadcast_to(
                    values[None], (copies, 1, lanes)
                )


def student_logits(where, head, teachers, arrays, origins, side, subs):
    blocks, v, d = head.shape
    toks, _, width = teachers.shape
    r = toks * width
    order = [i % toks * subs + i // toks for i in range(blocks)]
    count = sum(len(steps) for steps, _, _ in origins)
    return pl.pallas_call(
        functools.partial(student_kernel, order, side, origins),
        in_specs=[SMEM] + [VMEM] * 2 + [HBM] * len(arrays),
        out_specs=[VMEM] * 3,
        out_shape=[
            jax.ShapeDtypeStruct((v, r), F32),
            jax.ShapeDtypeStruct((blocks, 3 * r // 128, 128), F32),
            jax.ShapeDtypeStruct((d, r), BF16),
        ],
        scratch_shapes=[pltpu.VMEM((blocks * d, r), BF16), pltpu.SemaphoreType.DMA((count,))],
        compiler_params=params(58),
        cost_estimate=pl.CostEstimate(
            flops=2 * r * v * d * blocks, bytes_accessed=12 * MIB, transcendentals=0
        ),
    )(where, head, teachers, *arrays)


def merge(stats):
    return jnp.concatenate(merged(stats))


def grad_kernel(
    where_ref, stats_ref, weight_ref, student_ref, teacher_ref, low_ref, high_ref, divergence_ref
):
    student_lse, teacher_lse, cross = merged(stats_ref[...])
    divergence = cross + student_lse - teacher_lse
    index = lax.broadcasted_iota(jnp.int32, divergence.shape, 0)
    divergence_ref[...] = jnp.sum(
        jnp.where(index == where_ref[0], divergence, 0.0), axis=0, keepdims=True
    )
    half, rows = low_ref.shape
    width = teacher_ref.shape[2]
    for j in range(rows // 128):
        cols = slice(j * 128, (j + 1) * 128)
        inner = slice(j * 128 % width, j * 128 % width + 128)
        teacher = teacher_ref[j * 128 // width, :, inner].astype(F32)
        grad = weight_ref[j : j + 1, :] * (
            jnp.exp(student_ref[:, cols] - student_lse[j : j + 1, :])
            - jnp.exp(teacher - teacher_lse[j : j + 1, :])
        )
        grad = grad.astype(BF16)
        low_ref[:, cols] = grad[:half]
        high_ref[:, cols] = grad[half:]


def logit_grads(where, stats, weights, student, teachers):
    v, r = student.shape
    return pl.pallas_call(
        grad_kernel,
        in_specs=[SMEM] + [VMEM] * 4,
        out_specs=[VMEM] * 3,
        out_shape=[
            jax.ShapeDtypeStruct((v // 2, r), BF16),
            jax.ShapeDtypeStruct((v // 2, r), BF16),
            jax.ShapeDtypeStruct((1, 128), F32),
        ],
        compiler_params=params(58),
    )(where, stats, weights, student, teachers)


def ring_slot(where_ref, back, ring):
    origin = lax.rem(where_ref[0] + ring - back, ring)
    return lax.rem(origin, 2) * (ring // 2) + origin // 2


def fetch_blocks(where_ref, block_refs, hops, all_ref, sem):
    height = block_refs[0].shape[0]
    ring = all_ref.shape[0] // (2 * height)
    copies = []
    for index, (block_ref, (back, half)) in enumerate(zip(block_refs, hops)):
        slot = ring_slot(where_ref, back, ring)
        start = pl.multiple_of(slot * (2 * height) + half * height, 16)
        copies.append(
            pltpu.make_async_copy(block_ref, all_ref.at[pl.ds(start, height)], sem.at[index])
        )
    for copy in copies:
        copy.start()
    for copy in copies:
        copy.wait()


def early_kernel(hops, where_ref, *refs):
    blocks, (head_ref, out_ref, all_ref, sem) = refs[: len(hops)], refs[len(hops) :]
    height = blocks[0].shape[0]
    ring = all_ref.shape[0] // (2 * height)
    for back in range(ring):
        if (back, 0) not in hops:
            missing = ring_slot(where_ref, back, ring) * (2 * height)
            empty = all_ref.at[pl.ds(pl.multiple_of(missing, 2 * height), 2 * height)]
            empty[...] = jnp.zeros(empty.shape, BF16)
    fetch_blocks(where_ref, blocks, hops, all_ref, sem)
    tile = 256

    @pl.loop(0, all_ref.shape[1] // tile)
    def _(i):
        rows = pl.ds(pl.multiple_of(i * tile, tile), tile)
        out_ref[rows, :] = jnp.dot(
            head_ref[...], all_ref[:, rows], preferred_element_type=F32
        ).T


def early_features(where, blocks, hops, head):
    depth, vocab = head.shape
    rows = blocks[0].shape[1]
    return pl.pallas_call(
        functools.partial(early_kernel, hops),
        in_specs=[SMEM] + [HBM] * len(blocks) + [VMEM],
        out_specs=VMEM,
        out_shape=jax.ShapeDtypeStruct((rows, depth), F32),
        scratch_shapes=[pltpu.VMEM((vocab, rows), BF16), pltpu.SemaphoreType.DMA((len(blocks),))],
        compiler_params=params(32),
        cost_estimate=pl.CostEstimate(
            flops=2 * rows * depth * vocab, bytes_accessed=8 * MIB, transcendentals=0
        ),
    )(where, *blocks, head)


def late_kernel(ring, hops, where_ref, *refs):
    block_refs, rest = refs[: len(hops)], refs[len(hops) :]
    head_ref, part_ref, keep_ref, give_ref, window, block, sem = rest
    height = block_refs[0].shape[0]
    backs = sorted({back for back, _ in hops})
    span = window.shape[1] // len(backs)
    gap = span - 2 * height
    copies = []
    for index, back in enumerate(backs):
        offset = ring_slot(where_ref, back, ring) * (2 * height)
        start = pl.multiple_of(offset // 128 * 128, 128)
        base = index * span
        copy = pltpu.make_async_copy(
            head_ref.at[:, pl.ds(start, span)], window.at[:, base : base + span], sem.at[index]
        )
        copy.start()
        copies.append(copy)
        block[base : base + gap] = jnp.zeros((gap, block.shape[1]), BF16)
        block[base + span - gap : base + span] = jnp.zeros((gap, block.shape[1]), BF16)
        for block_ref, hop in zip(block_refs, hops):
            if hop[0] == back:
                at = pl.multiple_of(base + offset - start + hop[1] * height, 32)
                block[pl.ds(at, height)] = block_ref[...]
    for copy in copies:
        copy.wait()
    first = where_ref[1] == 0
    tile = 256
    per = keep_ref.shape[1]
    chips = tile // (2 * per)

    @pl.loop(0, block.shape[1] // tile)
    def _(i):
        rows = pl.ds(pl.multiple_of(i * tile, tile), tile)
        part = jnp.dot(window[...], block[:, rows], preferred_element_type=F32).T
        part = part + part_ref[rows, :]
        part = part.reshape(chips, 2, per, part.shape[1])
        even, odd = part[:, 0], part[:, 1]
        keep_ref[pl.ds(i * chips, chips)] = jnp.where(first, even, odd)
        give_ref[pl.ds(i * chips, chips)] = jnp.where(first, odd, even)


def late_features(where, blocks, hops, head, part, ring, per):
    depth, _ = head.shape
    height, rows = blocks[0].shape
    count = len({back for back, _ in hops})
    span = -(-2 * height // 128) * 128
    shape = jax.ShapeDtypeStruct((rows // (2 * per), per, depth), F32)
    return pl.pallas_call(
        functools.partial(late_kernel, ring, hops),
        in_specs=[SMEM] + [VMEM] * len(blocks) + [HBM, VMEM],
        out_specs=[VMEM] * 2,
        out_shape=[shape, shape],
        scratch_shapes=[
            pltpu.VMEM((depth, count * span), BF16),
            pltpu.VMEM((count * span, rows), BF16),
            pltpu.SemaphoreType.DMA((count,)),
        ],
        compiler_params=params(32),
        cost_estimate=pl.CostEstimate(
            flops=2 * rows * depth * span * count, bytes_accessed=6 * MIB, transcendentals=0
        ),
    )(where, *blocks, head, part)


def head_kernel(hops, where_ref, *refs):
    blocks, rest = refs[: len(hops)], refs[len(hops) :]
    features_ref, out_ref, own_ref, all_ref, sem = rest
    step = pl.program_id(0)

    @pl.when(step == 0)
    def _():
        fetch_blocks(where_ref, blocks, hops, all_ref, sem)

    share, tile = own_ref.shape
    own_cols = pl.ds(pl.multiple_of(where_ref[0] * share, share), share)
    rows = pl.ds(pl.multiple_of(step * tile, tile), tile)
    out_ref[...] = lax.dot_general(
        features_ref[...], all_ref[rows, :], (((1,), (1,)), ((), ())), preferred_element_type=F32
    )
    own_ref[...] = all_ref[rows, own_cols].astype(F32).T.astype(BF16)


def head_parts(where, blocks, hops, features, vocab, share):
    depth, rows = features.shape
    tile = 512
    return pl.pallas_call(
        functools.partial(head_kernel, hops),
        grid=(vocab // tile,),
        in_specs=[SMEM] + [HBM] * len(blocks) + [pl.BlockSpec((depth, rows), lambda i: (0, 0))],
        out_specs=[
            pl.BlockSpec((depth, tile), lambda i: (0, i)),
            pl.BlockSpec((share, tile), lambda i: (0, i)),
        ],
        out_shape=[
            jax.ShapeDtypeStruct((depth, vocab), F32),
            jax.ShapeDtypeStruct((share, vocab), BF16),
        ],
        scratch_shapes=[
            pltpu.VMEM((vocab, rows), BF16),
            pltpu.SemaphoreType.DMA((len(blocks),)),
        ],
        compiler_params=params(58),
        cost_estimate=pl.CostEstimate(
            flops=2 * rows * depth * vocab, bytes_accessed=12 * MIB, transcendentals=0
        ),
    )(where, *blocks, features)


def ring_shift(values, step, size):
    return lax.ppermute(values, RING, [(i, (i + step) % size) for i in range(size)])


def ring_gather(halves, size):
    blocks, hops = list(halves), [(0, 0), (0, 1)]
    ahead, behind = list(halves), list(halves)
    for step in range(1, size // 2 + 1):
        last = step == size // 2
        for half in range(2):
            if not last or half == 1:
                ahead[half] = ring_shift(ahead[half], 1, size)
                blocks.append(ahead[half])
                hops.append((step, half))
            if not last or half == 0:
                behind[half] = ring_shift(behind[half], -1, size)
                blocks.append(behind[half])
                hops.append((size - step, half))
    return blocks, hops


def to_all(values, axis, **groups):
    size = lax.axis_size(axis)
    if groups:
        size = len(groups["axis_index_groups"][0])
    return lax.all_to_all(jnp.broadcast_to(values[None], (size,) + values.shape), axis, 0, 0, **groups)


def spread(column, chips_x, chips_y):
    def shift(values, x, y, core):
        pairs = []
        for i in range(chips_x):
            for j in range(chips_y):
                for c in range(2):
                    target = ((i + x) % chips_x * chips_y + (j + y) % chips_y) * 2 + (c ^ core)
                    pairs.append(((i * chips_y + j) * 2 + c, target))
        return lax.ppermute(values, "voc", pairs)

    half = column.shape[0] // 2
    first, second = column[:half], column[half:]
    along_x = [first] + [shift(first, k, 0, 0) for k in range(1, chips_x)]
    along_y = [second] + [shift(second, 0, k, 0) for k in range(1, chips_y)]
    along_x, along_y = lax.optimization_barrier((along_x, along_y))
    first, second = jnp.concatenate(along_x), jnp.concatenate(along_y)
    arrays = [(first, [(i, 0) for i in range(chips_x)], 0), (second, [(0, i) for i in range(chips_y)], 1)]
    for k in range(1, max(chips_x, chips_y)):
        if k < chips_y:
            arrays.append((shift(first, 0, k, 0), [(i, k) for i in range(chips_x)], 0))
        if k < chips_x:
            arrays.append((shift(second, k, 0, 0), [(k, i) for i in range(chips_y)], 1))
    out, origins = [], []
    for values, steps, which in arrays:
        out += [values, shift(values, 0, 0, 1)]
        origins += [(steps, 0, which), (steps, 1, which)]
    return out, origins


def on_device(hidden, head, pool, lines, sizes):
    toks, subs, vocs = lax.axis_size("tok"), lax.axis_size("sub"), lax.axis_size("voc")
    ring = toks * subs
    chips = vocs // 2
    share, width = hidden.shape
    rows = share * ring
    depth, vocab = head.shape
    cut = vocab // ring
    kept = lines.shape[0]
    tok = lax.axis_index("tok")
    place = lax.axis_index(RING)
    voc = lax.axis_index("voc")
    where = jnp.stack([place, voc % 2, voc])
    cores = [(i, i ^ 1) for i in range(vocs)]
    groups = [[2 * i + c for i in range(chips)] for c in range(2)]

    wanted = lines - tok * pool.shape[0]
    choose = (
        lax.broadcasted_iota(jnp.int32, (pool.shape[0], kept), 0) == wanted[None, :]
    ).astype(BF16)
    picked = lax.dot_general(
        pool, choose, (((0,), (0,)), ((), ())), preferred_element_type=F32
    ).astype(BF16).reshape(toks, cut, kept)
    parts = []
    for shift in range(toks):
        part = lax.dynamic_index_in_dim(picked, (tok + shift) % toks, 0, keepdims=False)
        if shift:
            part = lax.ppermute(part, "tok", [(i, (i + shift) % toks) for i in range(toks)])
        parts.append(part)

    piece = width // vocs
    own = lax.dynamic_slice_in_dim(hidden, voc * piece, piece, 1)
    column = to_all(own, RING)
    slices = head.T.reshape(ring, cut, depth)
    slices, column, *parts = lax.optimization_barrier((slices, column, *parts))
    side = math.isqrt(chips)
    arrays, origins = spread(column.reshape(rows, piece).T, side, side)
    head_cut = lax.all_to_all(slices, ("sub", "tok"), 0, 0)
    teachers = jnp.zeros((toks, cut, kept), BF16)
    for shift, part in enumerate(parts):
        teachers = lax.dynamic_update_index_in_dim(teachers, part, (tok + toks - shift) % toks, 0)
    weights = row_weights(sizes, rows).reshape(rows // 128, 128)

    student, stats, features = student_logits(
        where, head_cut, teachers, arrays, origins, side, subs
    )
    stats = merge(lax.all_to_all(stats, RING, 0, 0))
    stats = merge(jnp.stack([stats, lax.ppermute(stats, "voc", cores)]))
    stats = jnp.broadcast_to(stats[None], (chips,) + stats.shape)
    stats = lax.all_to_all(stats, "voc", 0, 0, axis_index_groups=groups)
    low, high, divergence = logit_grads(where, stats, weights, student, teachers)
    blocks, hops = ring_gather((low, high), ring)

    part = early_features(where, blocks[:-6], hops[:-6], head)
    keep, give = late_features(where, blocks[-6:], hops[-6:], head, part, ring, rows // vocs)
    given = lax.ppermute(give, "voc", cores)
    sums, where = lax.optimization_barrier(((keep + given).astype(BF16), where))
    sums = lax.all_to_all(sums, "voc", 0, 0, axis_index_groups=groups)
    feature_grad = jnp.sum(sums.astype(F32), axis=0)

    head_grad, local_grad = head_parts(where, blocks, hops, features, vocab, share)
    return head_grad, feature_grad, local_grad, divergence.reshape(share)


def solution(mesh):
    return jax.shard_map(
        on_device,
        mesh=mesh,
        in_specs=(
            P(RING, None),
            P(RING, "voc"),
            P("tok", ("voc", "sub")),
            P("tok"),
            P(),
        ),
        out_specs=(
            P(RING, "voc"),
            P("voc", RING),
            P(RING, "voc"),
            P(RING),
        ),
        check_vma=False,
    )
```

```python
import functools
import math

import jax
import jax.numpy as jnp
from jax import lax
from jax.experimental import pallas as pl
from jax.experimental.pallas import tpu as pltpu
from jax.sharding import PartitionSpec as P

LOSS_SCALE = 65536
F32 = jnp.float32
BF16 = jnp.bfloat16
RING = ("tok", "sub")


def row_weights(sizes, rows):
    count = sizes.shape[0]
    upto = lax.broadcasted_iota(jnp.int32, (count, count), 0) <= lax.broadcasted_iota(
        jnp.int32, (count, count), 1
    )
    ends = jnp.sum(jnp.where(upto, sizes[:, None], 0), axis=0)
    starts = ends - sizes
    ids = lax.broadcasted_iota(jnp.int32, (count, rows), 1)
    member = (ids >= starts[:, None]) & (ids < ends[:, None])
    lengths = jnp.sum(jnp.where(member, sizes[:, None], 0), axis=0).astype(F32)
    return F32(LOSS_SCALE) / (F32(count) * lengths)


MIB = 1024 * 1024
VMEM = pl.BlockSpec(memory_space=pltpu.VMEM)
SMEM = pl.BlockSpec(memory_space=pltpu.SMEM)
HBM = pl.BlockSpec(memory_space=pl.ANY)


def params(mib):
    return pltpu.CompilerParams(vmem_limit_bytes=mib * MIB)


def log_sum_exp(values):
    top = jnp.max(values, axis=0, keepdims=True)
    return top + jnp.log(jnp.sum(jnp.exp(values - top), axis=0, keepdims=True))


def merged(stats):
    k = stats.shape[1] // 3
    student, teacher, cross = stats[:, :k], stats[:, k : 2 * k], stats[:, 2 * k :]
    student_lse, teacher_lse = log_sum_exp(student), log_sum_exp(teacher)
    cross = jnp.sum(jnp.exp(teacher - teacher_lse) * cross, axis=0)
    return student_lse[0], teacher_lse[0], cross


def stack_kernel(where_ref, *refs):
    parts, out_ref = refs[:-1], refs[-1]
    toks = len(parts)
    for shift, part in enumerate(parts):
        out_ref[lax.rem(where_ref[3] + toks - shift, toks)] = part[...]


def stack_teachers(where, parts):
    return pl.pallas_call(
        stack_kernel,
        in_specs=[SMEM] + [VMEM] * len(parts),
        out_specs=VMEM,
        out_shape=jax.ShapeDtypeStruct((len(parts),) + parts[0].shape, BF16),
        compiler_params=params(24),
        cost_estimate=pl.CostEstimate(
            flops=40_000_000_000, bytes_accessed=2 * MIB, transcendentals=0
        ),
    )(where, *parts)


def place_columns(voc, side, array_refs, origins, out_ref, sem):
    core, chip = lax.rem(voc, 2), voc // 2
    x, y = chip // side, lax.rem(chip, side)
    copies = []
    for number, (array_ref, (steps, other, which)) in enumerate(zip(array_refs, origins)):
        height, width = array_ref.shape[0] // len(steps), array_ref.shape[1]
        for index, (back_x, back_y) in enumerate(steps):
            from_x = lax.rem(x + side - back_x, side)
            from_y = lax.rem(y + side - back_y, side)
            from_core = 1 - core if other else core
            start = ((from_x * side + from_y) * 2 + from_core) * height
            copy = pltpu.make_async_copy(
                array_ref.at[index * height : (index + 1) * height],
                out_ref.at[pl.ds(pl.multiple_of(start, height), height), which * width : (which + 1) * width],
                sem.at[index, number],
            )
            copy.start()
            copies.append((which, copy))
    return copies


def assemble_kernel(side, origins, where_ref, *refs):
    arrays, (out_ref, own_ref, sem) = refs[: len(origins)], refs[len(origins) :]
    for _, copy in place_columns(where_ref[2], side, arrays, origins, out_ref, sem):
        copy.wait()
    depth = own_ref.shape[0]
    own_ref[...] = out_ref[pl.ds(pl.multiple_of(where_ref[0] * depth, depth), depth), :]


def assemble(where, arrays, origins, side, depth):
    height = len(origins[0][0]) * len(arrays) // 2 * (arrays[0].shape[0] // len(origins[0][0]))
    rows = 2 * arrays[0].shape[1]
    return pl.pallas_call(
        functools.partial(assemble_kernel, side, origins),
        in_specs=[SMEM] + [HBM] * len(arrays),
        out_specs=[VMEM] * 2,
        out_shape=[
            jax.ShapeDtypeStruct((height, rows), BF16),
            jax.ShapeDtypeStruct((depth, rows), BF16),
        ],
        scratch_shapes=[pltpu.SemaphoreType.DMA((len(origins[0][0]), len(arrays)))],
        compiler_params=params(40),
        cost_estimate=pl.CostEstimate(flops=0, bytes_accessed=0, transcendentals=0),
    )(where, *arrays)


def student_kernel(order, head_hbm, features_ref, teacher_ref, student_ref, stats_ref, head_ref, sem):
    depth = head_hbm.shape[2]
    head_copies = [
        pltpu.make_async_copy(
            head_hbm.at[index], head_ref.at[:, block * depth : (block + 1) * depth], sem.at[index]
        )
        for index, block in enumerate(order)
    ]
    for copy in head_copies:
        copy.start()
    for copy in head_copies:
        copy.wait()
    student_ref[...] = jnp.dot(head_ref[...], features_ref[...], preferred_element_type=F32)
    copies, height, lanes = stats_ref.shape
    toks, _, width = teacher_ref.shape
    for i in range(toks):
        student = student_ref[:, i * width : (i + 1) * width]
        teacher = teacher_ref[i].astype(F32)
        student_lse, teacher_lse = log_sum_exp(student), log_sum_exp(teacher)
        cross = jnp.sum(
            jnp.exp(teacher - teacher_lse) * (teacher - student), axis=0, keepdims=True
        )
        pieces = width // lanes
        for index, row in enumerate((student_lse, teacher_lse, cross)):
            for piece in range(pieces):
                place = index * (height // 3) + i * pieces + piece
                values = row[:, piece * lanes : (piece + 1) * lanes]
                stats_ref[:, place : place + 1, :] = jnp.broadcast_to(
                    values[None], (copies, 1, lanes)
                )


def student_logits(head, features, teachers, subs):
    blocks, v, d = head.shape
    toks = teachers.shape[0]
    r = features.shape[1]
    order = [i % toks * subs + i // toks for i in range(blocks)]
    return pl.pallas_call(
        functools.partial(student_kernel, order),
        in_specs=[HBM, VMEM, VMEM],
        out_specs=[VMEM] * 2,
        out_shape=[
            jax.ShapeDtypeStruct((v, r), F32),
            jax.ShapeDtypeStruct((2 * blocks, 3 * r // 128, 128), F32),
        ],
        scratch_shapes=[pltpu.VMEM((v, blocks * d), BF16), pltpu.SemaphoreType.DMA((blocks,))],
        compiler_params=params(20),
        cost_estimate=pl.CostEstimate(
            flops=2 * r * v * d * blocks, bytes_accessed=12 * MIB, transcendentals=0
        ),
    )(head, features, teachers)


def merge(stats):
    return jnp.concatenate(merged(stats))


def grad_kernel(
    where_ref, stats_ref, weight_ref, student_ref, teacher_ref, low_ref, high_ref, divergence_ref
):
    student_lse, teacher_lse, cross = merged(stats_ref[...])
    divergence = cross + student_lse - teacher_lse
    index = lax.broadcasted_iota(jnp.int32, divergence.shape, 0)
    divergence_ref[...] = jnp.sum(
        jnp.where(index == where_ref[0], divergence, 0.0), axis=0, keepdims=True
    )
    half, rows = low_ref.shape
    width = teacher_ref.shape[2]
    for j in range(rows // 128):
        cols = slice(j * 128, (j + 1) * 128)
        inner = slice(j * 128 % width, j * 128 % width + 128)
        teacher = teacher_ref[j * 128 // width, :, inner].astype(F32)
        grad = weight_ref[j : j + 1, :] * (
            jnp.exp(student_ref[:, cols] - student_lse[j : j + 1, :])
            - jnp.exp(teacher - teacher_lse[j : j + 1, :])
        )
        grad = grad.astype(BF16)
        low_ref[:, cols] = grad[:half]
        high_ref[:, cols] = grad[half:]


def logit_grads(where, stats, weights, student, teachers):
    v, r = student.shape
    return pl.pallas_call(
        grad_kernel,
        in_specs=[SMEM] + [VMEM] * 4,
        out_specs=[VMEM] * 3,
        out_shape=[
            jax.ShapeDtypeStruct((v // 2, r), BF16),
            jax.ShapeDtypeStruct((v // 2, r), BF16),
            jax.ShapeDtypeStruct((1, 128), F32),
        ],
        compiler_params=params(20),
    )(where, stats, weights, student, teachers)


def ring_slot(where_ref, back, ring):
    origin = lax.rem(where_ref[0] + ring - back, ring)
    return lax.rem(origin, 2) * (ring // 2) + origin // 2


def fetch_blocks(where_ref, block_refs, hops, all_ref, sem):
    height = block_refs[0].shape[0]
    ring = all_ref.shape[0] // (2 * height)
    copies = []
    for index, (block_ref, (back, half)) in enumerate(zip(block_refs, hops)):
        slot = ring_slot(where_ref, back, ring)
        start = pl.multiple_of(slot * (2 * height) + half * height, 16)
        copies.append(
            pltpu.make_async_copy(block_ref, all_ref.at[pl.ds(start, height)], sem.at[index])
        )
    for copy in copies:
        copy.start()
    for copy in copies:
        copy.wait()


def early_kernel(hops, where_ref, *refs):
    blocks, (head_ref, out_ref, all_ref, sem) = refs[: len(hops)], refs[len(hops) :]
    height = blocks[0].shape[0]
    ring = all_ref.shape[0] // (2 * height)
    for back in range(ring):
        if (back, 0) not in hops:
            missing = ring_slot(where_ref, back, ring) * (2 * height)
            empty = all_ref.at[pl.ds(pl.multiple_of(missing, 2 * height), 2 * height)]
            empty[...] = jnp.zeros(empty.shape, BF16)
    fetch_blocks(where_ref, blocks, hops, all_ref, sem)
    tile = 256

    @pl.loop(0, all_ref.shape[1] // tile)
    def _(i):
        rows = pl.ds(pl.multiple_of(i * tile, tile), tile)
        out_ref[rows, :] = jnp.dot(
            head_ref[...], all_ref[:, rows], preferred_element_type=F32
        ).T


def early_features(where, blocks, hops, head):
    depth, vocab = head.shape
    rows = blocks[0].shape[1]
    return pl.pallas_call(
        functools.partial(early_kernel, hops),
        in_specs=[SMEM] + [HBM] * len(blocks) + [VMEM],
        out_specs=VMEM,
        out_shape=jax.ShapeDtypeStruct((rows, depth), F32),
        scratch_shapes=[pltpu.VMEM((vocab, rows), BF16), pltpu.SemaphoreType.DMA((len(blocks),))],
        compiler_params=params(32),
        cost_estimate=pl.CostEstimate(
            flops=2 * rows * depth * vocab, bytes_accessed=8 * MIB, transcendentals=0
        ),
    )(where, *blocks, head)


def late_kernel(ring, hops, where_ref, *refs):
    block_refs, rest = refs[: len(hops)], refs[len(hops) :]
    head_ref, part_ref, keep_ref, give_ref, window, block, sem = rest
    height = block_refs[0].shape[0]
    backs = sorted({back for back, _ in hops})
    span = window.shape[1] // len(backs)
    gap = span - 2 * height
    copies = []
    for index, back in enumerate(backs):
        offset = ring_slot(where_ref, back, ring) * (2 * height)
        start = pl.multiple_of(offset // 128 * 128, 128)
        base = index * span
        copy = pltpu.make_async_copy(
            head_ref.at[:, pl.ds(start, span)], window.at[:, base : base + span], sem.at[index]
        )
        copy.start()
        copies.append(copy)
        block[base : base + gap] = jnp.zeros((gap, block.shape[1]), BF16)
        block[base + span - gap : base + span] = jnp.zeros((gap, block.shape[1]), BF16)
        for block_ref, hop in zip(block_refs, hops):
            if hop[0] == back:
                at = pl.multiple_of(base + offset - start + hop[1] * height, 32)
                block[pl.ds(at, height)] = block_ref[...]
    for copy in copies:
        copy.wait()
    first = where_ref[1] == 0
    tile = 256
    per = keep_ref.shape[1]
    chips = tile // (2 * per)

    @pl.loop(0, block.shape[1] // tile)
    def _(i):
        rows = pl.ds(pl.multiple_of(i * tile, tile), tile)
        part = jnp.dot(window[...], block[:, rows], preferred_element_type=F32).T
        part = part + part_ref[rows, :]
        part = part.reshape(chips, 2, per, part.shape[1])
        even, odd = part[:, 0], part[:, 1]
        keep_ref[pl.ds(i * chips, chips)] = jnp.where(first, even, odd)
        give_ref[pl.ds(i * chips, chips)] = jnp.where(first, odd, even)


def late_features(where, blocks, hops, head, part, ring, per):
    depth, _ = head.shape
    height, rows = blocks[0].shape
    count = len({back for back, _ in hops})
    span = -(-2 * height // 128) * 128
    shape = jax.ShapeDtypeStruct((rows // (2 * per), per, depth), F32)
    return pl.pallas_call(
        functools.partial(late_kernel, ring, hops),
        in_specs=[SMEM] + [VMEM] * len(blocks) + [HBM, VMEM],
        out_specs=[VMEM] * 2,
        out_shape=[shape, shape],
        scratch_shapes=[
            pltpu.VMEM((depth, count * span), BF16),
            pltpu.VMEM((count * span, rows), BF16),
            pltpu.SemaphoreType.DMA((count,)),
        ],
        compiler_params=params(32),
        cost_estimate=pl.CostEstimate(
            flops=2 * rows * depth * span * count, bytes_accessed=6 * MIB, transcendentals=0
        ),
    )(where, *blocks, head, part)


def head_kernel(hops, where_ref, *refs):
    blocks, rest = refs[: len(hops)], refs[len(hops) :]
    features_ref, out_ref, own_ref, all_ref, sem = rest
    step = pl.program_id(0)

    @pl.when(step == 0)
    def _():
        fetch_blocks(where_ref, blocks, hops, all_ref, sem)

    share, tile = own_ref.shape
    own_cols = pl.ds(pl.multiple_of(where_ref[0] * share, share), share)
    rows = pl.ds(pl.multiple_of(step * tile, tile), tile)
    out_ref[...] = lax.dot_general(
        features_ref[...], all_ref[rows, :], (((1,), (1,)), ((), ())), preferred_element_type=F32
    )
    own_ref[...] = all_ref[rows, own_cols].astype(F32).T.astype(BF16)


def head_parts(where, blocks, hops, features, vocab, share):
    depth, rows = features.shape
    tile = 512
    return pl.pallas_call(
        functools.partial(head_kernel, hops),
        grid=(vocab // tile,),
        in_specs=[SMEM] + [HBM] * len(blocks) + [pl.BlockSpec((depth, rows), lambda i: (0, 0))],
        out_specs=[
            pl.BlockSpec((depth, tile), lambda i: (0, i)),
            pl.BlockSpec((share, tile), lambda i: (0, i)),
        ],
        out_shape=[
            jax.ShapeDtypeStruct((depth, vocab), F32),
            jax.ShapeDtypeStruct((share, vocab), BF16),
        ],
        scratch_shapes=[
            pltpu.VMEM((vocab, rows), BF16),
            pltpu.SemaphoreType.DMA((len(blocks),)),
        ],
        compiler_params=params(58),
        cost_estimate=pl.CostEstimate(
            flops=2 * rows * depth * vocab, bytes_accessed=12 * MIB, transcendentals=0
        ),
    )(where, *blocks, features)


def ring_shift(values, step, size):
    return lax.ppermute(values, RING, [(i, (i + step) % size) for i in range(size)])


def ring_gather(halves, size):
    blocks, hops = list(halves), [(0, 0), (0, 1)]
    ahead, behind = list(halves), list(halves)
    for step in range(1, size // 2 + 1):
        last = step == size // 2
        for half in range(2):
            if not last or half == 1:
                ahead[half] = ring_shift(ahead[half], 1, size)
                blocks.append(ahead[half])
                hops.append((step, half))
            if not last or half == 0:
                behind[half] = ring_shift(behind[half], -1, size)
                blocks.append(behind[half])
                hops.append((size - step, half))
    return blocks, hops


def to_all(values, axis, **groups):
    size = lax.axis_size(axis)
    if groups:
        size = len(groups["axis_index_groups"][0])
    return lax.all_to_all(jnp.broadcast_to(values[None], (size,) + values.shape), axis, 0, 0, **groups)


def spread(column, chips_x, chips_y):
    def shift(values, x, y, core):
        pairs = []
        for i in range(chips_x):
            for j in range(chips_y):
                for c in range(2):
                    target = ((i + x) % chips_x * chips_y + (j + y) % chips_y) * 2 + (c ^ core)
                    pairs.append(((i * chips_y + j) * 2 + c, target))
        return lax.ppermute(values, "voc", pairs)

    half = column.shape[1] // 2
    first, second = column[:, :half], column[:, half:]
    along_x = [first] + [shift(first, k, 0, 0) for k in range(1, chips_x)]
    along_y = [second] + [shift(second, 0, k, 0) for k in range(1, chips_y)]
    along_x, along_y = lax.optimization_barrier((along_x, along_y))
    first, second = jnp.concatenate(along_x), jnp.concatenate(along_y)
    arrays = [(first, [(i, 0) for i in range(chips_x)], 0), (second, [(0, i) for i in range(chips_y)], 1)]
    for k in range(1, max(chips_x, chips_y)):
        if k < chips_y:
            arrays.append((shift(first, 0, k, 0), [(i, k) for i in range(chips_x)], 0))
        if k < chips_x:
            arrays.append((shift(second, k, 0, 0), [(k, i) for i in range(chips_y)], 1))
    values = lax.optimization_barrier([array for array, _, _ in arrays])
    out, origins = [], []
    for (_, steps, which), value in zip(arrays, values):
        out += [value, shift(value, 0, 0, 1)]
        origins += [(steps, 0, which), (steps, 1, which)]
    return out, origins


def on_device(hidden, head, pool, lines, sizes):
    toks, subs, vocs = lax.axis_size("tok"), lax.axis_size("sub"), lax.axis_size("voc")
    ring = toks * subs
    chips = vocs // 2
    share, width = hidden.shape
    rows = share * ring
    depth, vocab = head.shape
    cut = vocab // ring
    kept = lines.shape[0]
    tok = lax.axis_index("tok")
    place = lax.axis_index(RING)
    voc = lax.axis_index("voc")
    where = jnp.stack([place, voc % 2, voc, tok])
    cores = [(i, i ^ 1) for i in range(vocs)]
    groups = [[2 * i + c for i in range(chips)] for c in range(2)]

    wanted = lines - tok * pool.shape[0]
    choose = (
        lax.broadcasted_iota(jnp.int32, (pool.shape[0], kept), 0) == wanted[None, :]
    ).astype(BF16)
    picked = lax.dot_general(
        pool, choose, (((0,), (0,)), ((), ())), preferred_element_type=F32
    ).astype(BF16).reshape(toks, cut, kept)
    parts = []
    for shift in range(toks):
        part = lax.dynamic_index_in_dim(picked, (tok + shift) % toks, 0, keepdims=False)
        if shift:
            part = lax.ppermute(part, "tok", [(i, (i + shift) % toks) for i in range(toks)])
        parts.append(part)

    piece = width // vocs
    own = lax.dynamic_slice_in_dim(hidden, voc * piece, piece, 1)
    column = to_all(own, RING)
    slices = head.T.reshape(ring, cut, depth)
    teachers = stack_teachers(where, parts)
    slices, column, teachers = lax.optimization_barrier((slices, column, teachers))
    side = math.isqrt(chips)
    arrays, origins = spread(column.reshape(rows, piece).T, side, side)
    features, own_features = assemble(where, arrays, origins, side, depth)
    head_cut = lax.all_to_all(slices, ("sub", "tok"), 0, 0)
    weights = row_weights(sizes, rows).reshape(rows // 128, 128)

    student, stats = student_logits(head_cut, features, teachers, subs)
    mixed = [
        [(t * vocs + 2 * i + c) * subs + u for t in range(toks) for c in range(2) for u in range(subs)]
        for i in range(chips)
    ]
    stats = merge(lax.all_to_all(stats, ("tok", "voc", "sub"), 0, 0, axis_index_groups=mixed))
    stats = jnp.broadcast_to(stats[None], (chips,) + stats.shape)
    stats = lax.all_to_all(stats, "voc", 0, 0, axis_index_groups=groups)
    low, high, divergence = logit_grads(where, stats, weights, student, teachers)
    blocks, hops = ring_gather((low, high), ring)

    part = early_features(where, blocks[:-6], hops[:-6], head)
    keep, give = late_features(where, blocks[-6:], hops[-6:], head, part, ring, rows // vocs)
    given = lax.ppermute(give, "voc", cores)
    sums, where = lax.optimization_barrier(((keep + given).astype(BF16), where))
    sums = lax.all_to_all(sums, "voc", 0, 0, axis_index_groups=groups)
    feature_grad = jnp.sum(sums.astype(F32), axis=0)

    head_grad, local_grad = head_parts(where, blocks, hops, own_features, vocab, share)
    return head_grad, feature_grad, local_grad, divergence.reshape(share)


def solution(mesh):
    return jax.shard_map(
        on_device,
        mesh=mesh,
        in_specs=(
            P(RING, None),
            P(RING, "voc"),
            P("tok", ("voc", "sub")),
            P("tok"),
            P(),
        ),
        out_specs=(
            P(RING, "voc"),
            P("voc", RING),
            P(RING, "voc"),
            P(RING),
        ),
        check_vma=False,
    )
```

```python
import functools
import math

import jax
import jax.numpy as jnp
from jax import lax
from jax.experimental import pallas as pl
from jax.experimental.pallas import tpu as pltpu
from jax.sharding import PartitionSpec as P

LOSS_SCALE = 65536
F32 = jnp.float32
BF16 = jnp.bfloat16
RING = ("tok", "sub")


def row_weights(sizes, rows):
    count = sizes.shape[0]
    upto = lax.broadcasted_iota(jnp.int32, (count, count), 0) <= lax.broadcasted_iota(
        jnp.int32, (count, count), 1
    )
    ends = jnp.sum(jnp.where(upto, sizes[:, None], 0), axis=0)
    starts = ends - sizes
    ids = lax.broadcasted_iota(jnp.int32, (count, rows), 1)
    member = (ids >= starts[:, None]) & (ids < ends[:, None])
    lengths = jnp.sum(jnp.where(member, sizes[:, None], 0), axis=0).astype(F32)
    return F32(LOSS_SCALE) / (F32(count) * lengths)


MIB = 1024 * 1024
VMEM = pl.BlockSpec(memory_space=pltpu.VMEM)
SMEM = pl.BlockSpec(memory_space=pltpu.SMEM)
HBM = pl.BlockSpec(memory_space=pl.ANY)


def params(mib):
    return pltpu.CompilerParams(vmem_limit_bytes=mib * MIB)


def log_sum_exp(values):
    top = jnp.max(values, axis=0, keepdims=True)
    return top + jnp.log(jnp.sum(jnp.exp(values - top), axis=0, keepdims=True))


def merged(stats):
    k = stats.shape[1] // 3
    student, teacher, cross = stats[:, :k], stats[:, k : 2 * k], stats[:, 2 * k :]
    student_lse, teacher_lse = log_sum_exp(student), log_sum_exp(teacher)
    cross = jnp.sum(jnp.exp(teacher - teacher_lse) * cross, axis=0)
    return student_lse[0], teacher_lse[0], cross


def stack_kernel(where_ref, *refs):
    parts, out_ref = refs[:-1], refs[-1]
    toks = len(parts)
    for shift, part in enumerate(parts):
        out_ref[lax.rem(where_ref[3] + toks - shift, toks)] = part[...]


def stack_teachers(where, parts):
    return pl.pallas_call(
        stack_kernel,
        in_specs=[SMEM] + [VMEM] * len(parts),
        out_specs=VMEM,
        out_shape=jax.ShapeDtypeStruct((len(parts),) + parts[0].shape, BF16),
        compiler_params=params(24),
        cost_estimate=pl.CostEstimate(
            flops=40_000_000_000, bytes_accessed=2 * MIB, transcendentals=0
        ),
    )(where, *parts)


def place_columns(voc, side, array_refs, origins, out_ref, sem):
    core, chip = lax.rem(voc, 2), voc // 2
    x, y = chip // side, lax.rem(chip, side)
    copies = []
    for number, (array_ref, (steps, other, which)) in enumerate(zip(array_refs, origins)):
        height, width = array_ref.shape[0] // len(steps), array_ref.shape[1]
        for index, (back_x, back_y) in enumerate(steps):
            from_x = lax.rem(x + side - back_x, side)
            from_y = lax.rem(y + side - back_y, side)
            from_core = 1 - core if other else core
            start = ((from_x * side + from_y) * 2 + from_core) * height
            copy = pltpu.make_async_copy(
                array_ref.at[index * height : (index + 1) * height],
                out_ref.at[pl.ds(pl.multiple_of(start, height), height), which * width : (which + 1) * width],
                sem.at[index, number],
            )
            copy.start()
            copies.append((which, copy))
    return copies


def assemble_kernel(side, origins, where_ref, *refs):
    arrays, (out_ref, sem) = refs[: len(origins)], refs[len(origins) :]
    for _, copy in place_columns(where_ref[2], side, arrays, origins, out_ref, sem):
        copy.wait()


def assemble(where, arrays, origins, side):
    height = len(origins[0][0]) * len(arrays) // 2 * (arrays[0].shape[0] // len(origins[0][0]))
    rows = 2 * arrays[0].shape[1]
    return pl.pallas_call(
        functools.partial(assemble_kernel, side, origins),
        in_specs=[SMEM] + [HBM] * len(arrays),
        out_specs=VMEM,
        out_shape=jax.ShapeDtypeStruct((height, rows), BF16),
        scratch_shapes=[pltpu.SemaphoreType.DMA((len(origins[0][0]), len(arrays)))],
        compiler_params=params(40),
        cost_estimate=pl.CostEstimate(flops=0, bytes_accessed=0, transcendentals=0),
    )(where, *arrays)


def student_kernel(order, head_hbm, features_ref, teacher_ref, student_ref, stats_ref, head_ref, sem):
    depth = head_hbm.shape[2]
    head_copies = [
        pltpu.make_async_copy(
            head_hbm.at[index], head_ref.at[:, block * depth : (block + 1) * depth], sem.at[index]
        )
        for index, block in enumerate(order)
    ]
    for copy in head_copies:
        copy.start()
    for copy in head_copies:
        copy.wait()
    student_ref[...] = jnp.dot(head_ref[...], features_ref[...], preferred_element_type=F32)
    copies, height, lanes = stats_ref.shape
    toks, _, width = teacher_ref.shape
    for i in range(toks):
        student = student_ref[:, i * width : (i + 1) * width]
        teacher = teacher_ref[i].astype(F32)
        student_lse, teacher_lse = log_sum_exp(student), log_sum_exp(teacher)
        cross = jnp.sum(
            jnp.exp(teacher - teacher_lse) * (teacher - student), axis=0, keepdims=True
        )
        pieces = width // lanes
        for index, row in enumerate((student_lse, teacher_lse, cross)):
            for piece in range(pieces):
                place = index * (height // 3) + i * pieces + piece
                values = row[:, piece * lanes : (piece + 1) * lanes]
                stats_ref[:, place : place + 1, :] = jnp.broadcast_to(
                    values[None], (copies, 1, lanes)
                )


def student_logits(head, features, teachers, subs):
    blocks, v, d = head.shape
    toks = teachers.shape[0]
    r = features.shape[1]
    order = [i % toks * subs + i // toks for i in range(blocks)]
    return pl.pallas_call(
        functools.partial(student_kernel, order),
        in_specs=[HBM, VMEM, VMEM],
        out_specs=[VMEM] * 2,
        out_shape=[
            jax.ShapeDtypeStruct((v, r), F32),
            jax.ShapeDtypeStruct((2 * blocks, 3 * r // 128, 128), F32),
        ],
        scratch_shapes=[pltpu.VMEM((v, blocks * d), BF16), pltpu.SemaphoreType.DMA((blocks,))],
        compiler_params=params(20),
        cost_estimate=pl.CostEstimate(
            flops=2 * r * v * d * blocks, bytes_accessed=12 * MIB, transcendentals=0
        ),
    )(head, features, teachers)


def merge(stats):
    return jnp.concatenate(merged(stats))


def grad_kernel(
    where_ref, stats_ref, weight_ref, student_ref, teacher_ref, low_ref, high_ref, divergence_ref
):
    student_lse, teacher_lse, cross = merged(stats_ref[...])
    divergence = cross + student_lse - teacher_lse
    index = lax.broadcasted_iota(jnp.int32, divergence.shape, 0)
    divergence_ref[...] = jnp.sum(
        jnp.where(index == where_ref[0], divergence, 0.0), axis=0, keepdims=True
    )
    half, rows = low_ref.shape
    width = teacher_ref.shape[2]
    for j in range(rows // 128):
        cols = slice(j * 128, (j + 1) * 128)
        inner = slice(j * 128 % width, j * 128 % width + 128)
        teacher = teacher_ref[j * 128 // width, :, inner].astype(F32)
        grad = weight_ref[j : j + 1, :] * (
            jnp.exp(student_ref[:, cols] - student_lse[j : j + 1, :])
            - jnp.exp(teacher - teacher_lse[j : j + 1, :])
        )
        grad = grad.astype(BF16)
        low_ref[:, cols] = grad[:half]
        high_ref[:, cols] = grad[half:]


def logit_grads(where, stats, weights, student, teachers):
    v, r = student.shape
    return pl.pallas_call(
        grad_kernel,
        in_specs=[SMEM] + [VMEM] * 4,
        out_specs=[VMEM] * 3,
        out_shape=[
            jax.ShapeDtypeStruct((v // 2, r), BF16),
            jax.ShapeDtypeStruct((v // 2, r), BF16),
            jax.ShapeDtypeStruct((1, 128), F32),
        ],
        compiler_params=params(20),
    )(where, stats, weights, student, teachers)


def ring_slot(where_ref, back, ring):
    origin = lax.rem(where_ref[0] + ring - back, ring)
    return lax.rem(origin, 2) * (ring // 2) + origin // 2


def fetch_blocks(where_ref, block_refs, hops, all_ref, sem):
    height = block_refs[0].shape[0]
    ring = all_ref.shape[0] // (2 * height)
    copies = []
    for index, (block_ref, (back, half)) in enumerate(zip(block_refs, hops)):
        slot = ring_slot(where_ref, back, ring)
        start = pl.multiple_of(slot * (2 * height) + half * height, 16)
        copies.append(
            pltpu.make_async_copy(block_ref, all_ref.at[pl.ds(start, height)], sem.at[index])
        )
    for copy in copies:
        copy.start()
    for copy in copies:
        copy.wait()


def early_kernel(hops, where_ref, *refs):
    blocks, (head_ref, out_ref, all_ref, sem) = refs[: len(hops)], refs[len(hops) :]
    height = blocks[0].shape[0]
    ring = all_ref.shape[0] // (2 * height)
    for back in range(ring):
        if (back, 0) not in hops:
            missing = ring_slot(where_ref, back, ring) * (2 * height)
            empty = all_ref.at[pl.ds(pl.multiple_of(missing, 2 * height), 2 * height)]
            empty[...] = jnp.zeros(empty.shape, BF16)
    fetch_blocks(where_ref, blocks, hops, all_ref, sem)
    tile = 256

    @pl.loop(0, all_ref.shape[1] // tile)
    def _(i):
        rows = pl.ds(pl.multiple_of(i * tile, tile), tile)
        out_ref[rows, :] = jnp.dot(
            head_ref[...], all_ref[:, rows], preferred_element_type=F32
        ).T


def early_features(where, blocks, hops, head):
    depth, vocab = head.shape
    rows = blocks[0].shape[1]
    return pl.pallas_call(
        functools.partial(early_kernel, hops),
        in_specs=[SMEM] + [HBM] * len(blocks) + [VMEM],
        out_specs=VMEM,
        out_shape=jax.ShapeDtypeStruct((rows, depth), F32),
        scratch_shapes=[pltpu.VMEM((vocab, rows), BF16), pltpu.SemaphoreType.DMA((len(blocks),))],
        compiler_params=params(32),
        cost_estimate=pl.CostEstimate(
            flops=2 * rows * depth * vocab, bytes_accessed=8 * MIB, transcendentals=0
        ),
    )(where, *blocks, head)


def late_kernel(ring, hops, where_ref, *refs):
    block_refs, rest = refs[: len(hops)], refs[len(hops) :]
    head_ref, part_ref, keep_ref, give_ref, window, block, sem = rest
    height = block_refs[0].shape[0]
    backs = sorted({back for back, _ in hops})
    span = window.shape[1] // len(backs)
    gap = span - 2 * height
    copies = []
    for index, back in enumerate(backs):
        offset = ring_slot(where_ref, back, ring) * (2 * height)
        start = pl.multiple_of(offset // 128 * 128, 128)
        base = index * span
        copy = pltpu.make_async_copy(
            head_ref.at[:, pl.ds(start, span)], window.at[:, base : base + span], sem.at[index]
        )
        copy.start()
        copies.append(copy)
        block[base : base + gap] = jnp.zeros((gap, block.shape[1]), BF16)
        block[base + span - gap : base + span] = jnp.zeros((gap, block.shape[1]), BF16)
        for block_ref, hop in zip(block_refs, hops):
            if hop[0] == back:
                at = pl.multiple_of(base + offset - start + hop[1] * height, 32)
                block[pl.ds(at, height)] = block_ref[...]
    for copy in copies:
        copy.wait()
    first = where_ref[1] == 0
    tile = 256
    per = keep_ref.shape[1]
    chips = tile // (2 * per)

    @pl.loop(0, block.shape[1] // tile)
    def _(i):
        rows = pl.ds(pl.multiple_of(i * tile, tile), tile)
        part = jnp.dot(window[...], block[:, rows], preferred_element_type=F32).T
        part = part + part_ref[rows, :]
        part = part.reshape(chips, 2, per, part.shape[1])
        even, odd = part[:, 0], part[:, 1]
        keep_ref[pl.ds(i * chips, chips)] = jnp.where(first, even, odd)
        give_ref[pl.ds(i * chips, chips)] = jnp.where(first, odd, even).astype(BF16)


def late_features(where, blocks, hops, head, part, ring, per):
    depth, _ = head.shape
    height, rows = blocks[0].shape
    count = len({back for back, _ in hops})
    span = -(-2 * height // 128) * 128
    shape = (rows // (2 * per), per, depth)
    return pl.pallas_call(
        functools.partial(late_kernel, ring, hops),
        in_specs=[SMEM] + [VMEM] * len(blocks) + [HBM, VMEM],
        out_specs=[VMEM] * 2,
        out_shape=[jax.ShapeDtypeStruct(shape, F32), jax.ShapeDtypeStruct(shape, BF16)],
        scratch_shapes=[
            pltpu.VMEM((depth, count * span), BF16),
            pltpu.VMEM((count * span, rows), BF16),
            pltpu.SemaphoreType.DMA((count,)),
        ],
        compiler_params=params(32),
        cost_estimate=pl.CostEstimate(
            flops=2 * rows * depth * span * count, bytes_accessed=6 * MIB, transcendentals=0
        ),
    )(where, *blocks, head, part)


def head_kernel(hops, where_ref, *refs):
    blocks, rest = refs[: len(hops)], refs[len(hops) :]
    features_hbm, out_ref, own_ref, all_ref, own_features, sem, own_sem = rest
    depth = own_features.shape[0]
    step = pl.program_id(0)

    @pl.when(step == 0)
    def _():
        mine = pl.ds(pl.multiple_of(where_ref[0] * depth, depth), depth)
        copy = pltpu.make_async_copy(features_hbm.at[mine], own_features, own_sem)
        copy.start()
        fetch_blocks(where_ref, blocks, hops, all_ref, sem)
        copy.wait()

    share, tile = own_ref.shape
    own_cols = pl.ds(pl.multiple_of(where_ref[0] * share, share), share)
    rows = pl.ds(pl.multiple_of(step * tile, tile), tile)
    out_ref[...] = lax.dot_general(
        own_features[...], all_ref[rows, :], (((1,), (1,)), ((), ())), preferred_element_type=F32
    )
    own_ref[...] = all_ref[rows, own_cols].astype(F32).T.astype(BF16)


def head_parts(where, blocks, hops, features, depth, vocab, share):
    rows = blocks[0].shape[1]
    tile = 512
    return pl.pallas_call(
        functools.partial(head_kernel, hops),
        grid=(vocab // tile,),
        in_specs=[SMEM] + [HBM] * (len(blocks) + 1),
        out_specs=[
            pl.BlockSpec((depth, tile), lambda i: (0, i)),
            pl.BlockSpec((share, tile), lambda i: (0, i)),
        ],
        out_shape=[
            jax.ShapeDtypeStruct((depth, vocab), F32),
            jax.ShapeDtypeStruct((share, vocab), BF16),
        ],
        scratch_shapes=[
            pltpu.VMEM((vocab, rows), BF16),
            pltpu.VMEM((depth, rows), BF16),
            pltpu.SemaphoreType.DMA((len(blocks),)),
            pltpu.SemaphoreType.DMA,
        ],
        compiler_params=params(58),
        cost_estimate=pl.CostEstimate(
            flops=2 * rows * depth * vocab, bytes_accessed=12 * MIB, transcendentals=0
        ),
    )(where, *blocks, features)


def ring_shift(values, step, size):
    return lax.ppermute(values, RING, [(i, (i + step) % size) for i in range(size)])


def ring_gather(halves, size):
    blocks, hops = list(halves), [(0, 0), (0, 1)]
    ahead, behind = list(halves), list(halves)
    for step in range(1, size // 2 + 1):
        last = step == size // 2
        for half in range(2):
            if not last or half == 1:
                ahead[half] = ring_shift(ahead[half], 1, size)
                blocks.append(ahead[half])
                hops.append((step, half))
            if not last or half == 0:
                behind[half] = ring_shift(behind[half], -1, size)
                blocks.append(behind[half])
                hops.append((size - step, half))
    return blocks, hops


def to_all(values, axis, **groups):
    size = lax.axis_size(axis)
    if groups:
        size = len(groups["axis_index_groups"][0])
    return lax.all_to_all(jnp.broadcast_to(values[None], (size,) + values.shape), axis, 0, 0, **groups)


def spread(column, chips_x, chips_y):
    def shift(values, x, y, core):
        pairs = []
        for i in range(chips_x):
            for j in range(chips_y):
                for c in range(2):
                    target = ((i + x) % chips_x * chips_y + (j + y) % chips_y) * 2 + (c ^ core)
                    pairs.append(((i * chips_y + j) * 2 + c, target))
        return lax.ppermute(values, "voc", pairs)

    half = column.shape[1] // 2
    first, second = column[:, :half], column[:, half:]
    along_x = [first] + [shift(first, k, 0, 0) for k in range(1, chips_x)]
    along_y = [second] + [shift(second, 0, k, 0) for k in range(1, chips_y)]
    along_x, along_y = lax.optimization_barrier((along_x, along_y))
    first, second = jnp.concatenate(along_x), jnp.concatenate(along_y)
    arrays = [(first, [(i, 0) for i in range(chips_x)], 0), (second, [(0, i) for i in range(chips_y)], 1)]
    for k in range(1, max(chips_x, chips_y)):
        if k < chips_y:
            arrays.append((shift(first, 0, k, 0), [(i, k) for i in range(chips_x)], 0))
        if k < chips_x:
            arrays.append((shift(second, k, 0, 0), [(k, i) for i in range(chips_y)], 1))
    values = lax.optimization_barrier([array for array, _, _ in arrays])
    out, origins = [], []
    for (_, steps, which), value in zip(arrays, values):
        out += [value, shift(value, 0, 0, 1)]
        origins += [(steps, 0, which), (steps, 1, which)]
    return out, origins


def on_device(hidden, head, pool, lines, sizes):
    toks, subs, vocs = lax.axis_size("tok"), lax.axis_size("sub"), lax.axis_size("voc")
    ring = toks * subs
    chips = vocs // 2
    share, width = hidden.shape
    rows = share * ring
    depth, vocab = head.shape
    cut = vocab // ring
    kept = lines.shape[0]
    tok = lax.axis_index("tok")
    place = lax.axis_index(RING)
    voc = lax.axis_index("voc")
    where = jnp.stack([place, voc % 2, voc, tok])
    cores = [(i, i ^ 1) for i in range(vocs)]
    groups = [[2 * i + c for i in range(chips)] for c in range(2)]

    wanted = lines - tok * pool.shape[0]
    choose = (
        lax.broadcasted_iota(jnp.int32, (pool.shape[0], kept), 0) == wanted[None, :]
    ).astype(BF16)
    picked = lax.dot_general(
        pool, choose, (((0,), (0,)), ((), ())), preferred_element_type=F32
    ).astype(BF16).reshape(toks, cut, kept)
    parts = []
    for shift in range(toks):
        part = lax.dynamic_index_in_dim(picked, (tok + shift) % toks, 0, keepdims=False)
        if shift:
            part = lax.ppermute(part, "tok", [(i, (i + shift) % toks) for i in range(toks)])
        parts.append(part)

    piece = width // vocs
    own = lax.dynamic_slice_in_dim(hidden, voc * piece, piece, 1)
    column = to_all(own, RING)
    slices = head.T.reshape(ring, cut, depth)
    teachers = stack_teachers(where, parts)
    slices, column, teachers = lax.optimization_barrier((slices, column, teachers))
    side = math.isqrt(chips)
    arrays, origins = spread(column.reshape(rows, piece).T, side, side)
    features = assemble(where, arrays, origins, side)
    head_cut = lax.all_to_all(slices, ("sub", "tok"), 0, 0)
    weights = row_weights(sizes, rows).reshape(rows // 128, 128)

    student, stats = student_logits(head_cut, features, teachers, subs)
    mixed = [
        [(t * vocs + 2 * i + c) * subs + u for t in range(toks) for c in range(2) for u in range(subs)]
        for i in range(chips)
    ]
    stats = merge(lax.all_to_all(stats, ("tok", "voc", "sub"), 0, 0, axis_index_groups=mixed))
    stats = jnp.broadcast_to(stats[None], (chips,) + stats.shape)
    stats = lax.all_to_all(stats, "voc", 0, 0, axis_index_groups=groups)
    low, high, divergence = logit_grads(where, stats, weights, student, teachers)
    blocks, hops = ring_gather((low, high), ring)

    part = early_features(where, blocks[:-6], hops[:-6], head)
    keep, give = late_features(where, blocks[-6:], hops[-6:], head, part, ring, rows // vocs)
    given = lax.ppermute(give, "voc", cores)
    sums, where = lax.optimization_barrier(((keep + given.astype(F32)).astype(BF16), where))
    sums = lax.all_to_all(sums, "voc", 0, 0, axis_index_groups=groups)
    feature_grad = jnp.sum(sums.astype(F32), axis=0)

    head_grad, local_grad = head_parts(where, blocks, hops, features, depth, vocab, share)
    return head_grad, feature_grad, local_grad, divergence.reshape(share)


def solution(mesh):
    return jax.shard_map(
        on_device,
        mesh=mesh,
        in_specs=(
            P(RING, None),
            P(RING, "voc"),
            P("tok", ("voc", "sub")),
            P("tok"),
            P(),
        ),
        out_specs=(
            P(RING, "voc"),
            P("voc", RING),
            P(RING, "voc"),
            P(RING),
        ),
        check_vma=False,
    )
```

```python
import functools
import math

import jax
import jax.numpy as jnp
from jax import lax
from jax.experimental import pallas as pl
from jax.experimental.pallas import tpu as pltpu
from jax.sharding import PartitionSpec as P

LOSS_SCALE = 65536
F32 = jnp.float32
BF16 = jnp.bfloat16
RING = ("tok", "sub")


def row_weights(sizes, rows):
    count = sizes.shape[0]
    upto = lax.broadcasted_iota(jnp.int32, (count, count), 0) <= lax.broadcasted_iota(
        jnp.int32, (count, count), 1
    )
    ends = jnp.sum(jnp.where(upto, sizes[:, None], 0), axis=0)
    starts = ends - sizes
    ids = lax.broadcasted_iota(jnp.int32, (count, rows), 1)
    member = (ids >= starts[:, None]) & (ids < ends[:, None])
    lengths = jnp.sum(jnp.where(member, sizes[:, None], 0), axis=0).astype(F32)
    return F32(LOSS_SCALE) / (F32(count) * lengths)


MIB = 1024 * 1024
VMEM = pl.BlockSpec(memory_space=pltpu.VMEM)
SMEM = pl.BlockSpec(memory_space=pltpu.SMEM)
HBM = pl.BlockSpec(memory_space=pl.ANY)


def params(mib):
    return pltpu.CompilerParams(vmem_limit_bytes=mib * MIB)


def log_sum_exp(values):
    top = jnp.max(values, axis=0, keepdims=True)
    return top + jnp.log(jnp.sum(jnp.exp(values - top), axis=0, keepdims=True))


def merged(stats):
    k = stats.shape[1] // 3
    student, teacher, cross = stats[:, :k], stats[:, k : 2 * k], stats[:, 2 * k :]
    student_lse, teacher_lse = log_sum_exp(student), log_sum_exp(teacher)
    cross = jnp.sum(jnp.exp(teacher - teacher_lse) * cross, axis=0)
    return student_lse[0], teacher_lse[0], cross


def stack_kernel(where_ref, *refs):
    parts, out_ref = refs[:-1], refs[-1]
    toks = len(parts)
    for shift, part in enumerate(parts):
        out_ref[lax.rem(where_ref[3] + toks - shift, toks)] = part[...]


def stack_teachers(where, parts):
    return pl.pallas_call(
        stack_kernel,
        in_specs=[SMEM] + [VMEM] * len(parts),
        out_specs=VMEM,
        out_shape=jax.ShapeDtypeStruct((len(parts),) + parts[0].shape, BF16),
        compiler_params=params(24),
        cost_estimate=pl.CostEstimate(
            flops=40_000_000_000, bytes_accessed=2 * MIB, transcendentals=0
        ),
    )(where, *parts)


def place_columns(voc, side, array_refs, origins, out_ref, sem):
    core, chip = lax.rem(voc, 2), voc // 2
    x, y = chip // side, lax.rem(chip, side)
    copies = []
    for number, (array_ref, (steps, other, which)) in enumerate(zip(array_refs, origins)):
        height, width = array_ref.shape[0] // len(steps), array_ref.shape[1]
        for index, (back_x, back_y) in enumerate(steps):
            from_x = lax.rem(x + side - back_x, side)
            from_y = lax.rem(y + side - back_y, side)
            from_core = 1 - core if other else core
            start = ((from_x * side + from_y) * 2 + from_core) * height
            copy = pltpu.make_async_copy(
                array_ref.at[index * height : (index + 1) * height],
                out_ref.at[pl.ds(pl.multiple_of(start, height), height), which * width : (which + 1) * width],
                sem.at[index, number],
            )
            copy.start()
            copies.append((which, copy))
    return copies


def assemble_kernel(side, origins, where_ref, *refs):
    arrays, (out_ref, sem) = refs[: len(origins)], refs[len(origins) :]
    for _, copy in place_columns(where_ref[2], side, arrays, origins, out_ref, sem):
        copy.wait()


def assemble(where, arrays, origins, side):
    height = len(origins[0][0]) * len(arrays) // 2 * (arrays[0].shape[0] // len(origins[0][0]))
    rows = 2 * arrays[0].shape[1]
    return pl.pallas_call(
        functools.partial(assemble_kernel, side, origins),
        in_specs=[SMEM] + [HBM] * len(arrays),
        out_specs=VMEM,
        out_shape=jax.ShapeDtypeStruct((height, rows), BF16),
        scratch_shapes=[pltpu.SemaphoreType.DMA((len(origins[0][0]), len(arrays)))],
        compiler_params=params(40),
        cost_estimate=pl.CostEstimate(flops=0, bytes_accessed=0, transcendentals=0),
    )(where, *arrays)


def student_kernel(order, head_hbm, features_ref, teacher_ref, student_ref, stats_ref, head_ref, sem):
    depth = head_hbm.shape[2]
    head_copies = [
        pltpu.make_async_copy(
            head_hbm.at[index], head_ref.at[:, block * depth : (block + 1) * depth], sem.at[index]
        )
        for index, block in enumerate(order)
    ]
    for copy in head_copies:
        copy.start()
    for copy in head_copies:
        copy.wait()
    student_ref[...] = jnp.dot(head_ref[...], features_ref[...], preferred_element_type=F32)
    copies, height, lanes = stats_ref.shape
    toks, _, width = teacher_ref.shape
    for i in range(toks):
        student = student_ref[:, i * width : (i + 1) * width]
        teacher = teacher_ref[i].astype(F32)
        student_lse, teacher_lse = log_sum_exp(student), log_sum_exp(teacher)
        cross = jnp.sum(
            jnp.exp(teacher - teacher_lse) * (teacher - student), axis=0, keepdims=True
        )
        pieces = width // lanes
        for index, row in enumerate((student_lse, teacher_lse, cross)):
            for piece in range(pieces):
                place = index * (height // 3) + i * pieces + piece
                values = row[:, piece * lanes : (piece + 1) * lanes]
                stats_ref[:, place : place + 1, :] = jnp.broadcast_to(
                    values[None], (copies, 1, lanes)
                )


def student_logits(head, features, teachers, subs):
    blocks, v, d = head.shape
    toks = teachers.shape[0]
    r = features.shape[1]
    order = [i % toks * subs + i // toks for i in range(blocks)]
    return pl.pallas_call(
        functools.partial(student_kernel, order),
        in_specs=[HBM, VMEM, VMEM],
        out_specs=[VMEM] * 2,
        out_shape=[
            jax.ShapeDtypeStruct((v, r), F32),
            jax.ShapeDtypeStruct((2 * blocks, 3 * r // 128, 128), F32),
        ],
        scratch_shapes=[pltpu.VMEM((v, blocks * d), BF16), pltpu.SemaphoreType.DMA((blocks,))],
        compiler_params=params(20),
        cost_estimate=pl.CostEstimate(
            flops=2 * r * v * d * blocks, bytes_accessed=12 * MIB, transcendentals=0
        ),
    )(head, features, teachers)


def merge(stats):
    return jnp.concatenate(merged(stats))


def grad_kernel(
    where_ref, stats_ref, weight_ref, student_ref, teacher_ref, low_ref, high_ref, divergence_ref
):
    student_lse, teacher_lse, cross = merged(stats_ref[...])
    divergence = cross + student_lse - teacher_lse
    index = lax.broadcasted_iota(jnp.int32, divergence.shape, 0)
    divergence_ref[...] = jnp.sum(
        jnp.where(index == where_ref[0], divergence, 0.0), axis=0, keepdims=True
    )
    half, rows = low_ref.shape
    width = teacher_ref.shape[2]
    for j in range(rows // 128):
        cols = slice(j * 128, (j + 1) * 128)
        inner = slice(j * 128 % width, j * 128 % width + 128)
        teacher = teacher_ref[j * 128 // width, :, inner].astype(F32)
        grad = weight_ref[j : j + 1, :] * (
            jnp.exp(student_ref[:, cols] - student_lse[j : j + 1, :])
            - jnp.exp(teacher - teacher_lse[j : j + 1, :])
        )
        grad = grad.astype(BF16)
        low_ref[:, cols] = grad[:half]
        high_ref[:, cols] = grad[half:]


def logit_grads(where, stats, weights, student, teachers):
    v, r = student.shape
    return pl.pallas_call(
        grad_kernel,
        in_specs=[SMEM] + [VMEM] * 4,
        out_specs=[VMEM] * 3,
        out_shape=[
            jax.ShapeDtypeStruct((v // 2, r), BF16),
            jax.ShapeDtypeStruct((v // 2, r), BF16),
            jax.ShapeDtypeStruct((1, 128), F32),
        ],
        compiler_params=params(20),
    )(where, stats, weights, student, teachers)


def ring_slot(where_ref, back, ring):
    origin = lax.rem(where_ref[0] + ring - back, ring)
    return lax.rem(origin, 2) * (ring // 2) + origin // 2


def fetch_blocks(where_ref, block_refs, hops, all_ref, sem):
    height = block_refs[0].shape[0]
    ring = all_ref.shape[0] // (2 * height)
    copies = []
    for index, (block_ref, (back, half)) in enumerate(zip(block_refs, hops)):
        slot = ring_slot(where_ref, back, ring)
        start = pl.multiple_of(slot * (2 * height) + half * height, 16)
        copies.append(
            pltpu.make_async_copy(block_ref, all_ref.at[pl.ds(start, height)], sem.at[index])
        )
    for copy in copies:
        copy.start()
    for copy in copies:
        copy.wait()


def early_kernel(hops, where_ref, *refs):
    blocks, (head_ref, out_ref, all_ref, sem) = refs[: len(hops)], refs[len(hops) :]
    height = blocks[0].shape[0]
    ring = all_ref.shape[0] // (2 * height)
    for back in range(ring):
        if (back, 0) not in hops:
            missing = ring_slot(where_ref, back, ring) * (2 * height)
            empty = all_ref.at[pl.ds(pl.multiple_of(missing, 2 * height), 2 * height)]
            empty[...] = jnp.zeros(empty.shape, BF16)
    fetch_blocks(where_ref, blocks, hops, all_ref, sem)
    tile = 256

    @pl.loop(0, all_ref.shape[1] // tile)
    def _(i):
        rows = pl.ds(pl.multiple_of(i * tile, tile), tile)
        out_ref[rows, :] = jnp.dot(
            head_ref[...], all_ref[:, rows], preferred_element_type=F32
        ).T


def early_features(where, blocks, hops, head):
    depth, vocab = head.shape
    rows = blocks[0].shape[1]
    return pl.pallas_call(
        functools.partial(early_kernel, hops),
        in_specs=[SMEM] + [HBM] * len(blocks) + [VMEM],
        out_specs=VMEM,
        out_shape=jax.ShapeDtypeStruct((rows, depth), F32),
        scratch_shapes=[pltpu.VMEM((vocab, rows), BF16), pltpu.SemaphoreType.DMA((len(blocks),))],
        compiler_params=params(32),
        cost_estimate=pl.CostEstimate(
            flops=2 * rows * depth * vocab, bytes_accessed=8 * MIB, transcendentals=0
        ),
    )(where, *blocks, head)


def late_kernel(ring, hops, where_ref, *refs):
    block_refs, rest = refs[: len(hops)], refs[len(hops) :]
    head_ref, part_ref, keep_ref, give_ref, window, block, sem = rest
    height = block_refs[0].shape[0]
    backs = sorted({back for back, _ in hops})
    span = window.shape[1] // len(backs)
    gap = span - 2 * height
    copies = []
    for index, back in enumerate(backs):
        offset = ring_slot(where_ref, back, ring) * (2 * height)
        start = pl.multiple_of(offset // 128 * 128, 128)
        base = index * span
        copy = pltpu.make_async_copy(
            head_ref.at[:, pl.ds(start, span)], window.at[:, base : base + span], sem.at[index]
        )
        copy.start()
        copies.append(copy)
        block[base : base + gap] = jnp.zeros((gap, block.shape[1]), BF16)
        block[base + span - gap : base + span] = jnp.zeros((gap, block.shape[1]), BF16)
        for block_ref, hop in zip(block_refs, hops):
            if hop[0] == back:
                at = pl.multiple_of(base + offset - start + hop[1] * height, 32)
                block[pl.ds(at, height)] = block_ref[...]
    for copy in copies:
        copy.wait()
    first = where_ref[1] == 0
    tile = 256
    per = keep_ref.shape[1]
    chips = tile // (2 * per)

    @pl.loop(0, block.shape[1] // tile)
    def _(i):
        rows = pl.ds(pl.multiple_of(i * tile, tile), tile)
        part = jnp.dot(window[...], block[:, rows], preferred_element_type=F32).T
        part = part + part_ref[rows, :]
        part = part.reshape(chips, 2, per, part.shape[1])
        even, odd = part[:, 0], part[:, 1]
        keep_ref[pl.ds(i * chips, chips)] = jnp.where(first, even, odd)
        give_ref[pl.ds(i * chips, chips)] = jnp.where(first, odd, even).astype(BF16)


def late_features(where, blocks, hops, head, part, ring, per):
    depth, _ = head.shape
    height, rows = blocks[0].shape
    count = len({back for back, _ in hops})
    span = -(-2 * height // 128) * 128
    shape = (rows // (2 * per), per, depth)
    return pl.pallas_call(
        functools.partial(late_kernel, ring, hops),
        in_specs=[SMEM] + [VMEM] * len(blocks) + [HBM, VMEM],
        out_specs=[VMEM] * 2,
        out_shape=[jax.ShapeDtypeStruct(shape, F32), jax.ShapeDtypeStruct(shape, BF16)],
        scratch_shapes=[
            pltpu.VMEM((depth, count * span), BF16),
            pltpu.VMEM((count * span, rows), BF16),
            pltpu.SemaphoreType.DMA((count,)),
        ],
        compiler_params=params(32),
        cost_estimate=pl.CostEstimate(
            flops=2 * rows * depth * span * count, bytes_accessed=6 * MIB, transcendentals=0
        ),
    )(where, *blocks, head, part)


def head_kernel(hops, where_ref, *refs):
    blocks, rest = refs[: len(hops)], refs[len(hops) :]
    features_hbm, out_ref, own_ref, all_ref, own_features, sem, own_sem = rest
    depth = own_features.shape[0]
    step = pl.program_id(0)

    @pl.when(step == 0)
    def _():
        mine = pl.ds(pl.multiple_of(where_ref[0] * depth, depth), depth)
        copy = pltpu.make_async_copy(features_hbm.at[mine], own_features, own_sem)
        copy.start()
        fetch_blocks(where_ref, blocks, hops, all_ref, sem)
        copy.wait()

    share, tile = own_ref.shape
    own_cols = pl.ds(pl.multiple_of(where_ref[0] * share, share), share)
    rows = pl.ds(pl.multiple_of(step * tile, tile), tile)
    out_ref[...] = lax.dot_general(
        own_features[...], all_ref[rows, :], (((1,), (1,)), ((), ())), preferred_element_type=F32
    )
    own_ref[...] = all_ref[rows, own_cols].astype(F32).T.astype(BF16)


def head_parts(where, blocks, hops, features, depth, vocab, share):
    rows = blocks[0].shape[1]
    tile = 512
    return pl.pallas_call(
        functools.partial(head_kernel, hops),
        grid=(vocab // tile,),
        in_specs=[SMEM] + [HBM] * (len(blocks) + 1),
        out_specs=[
            pl.BlockSpec((depth, tile), lambda i: (0, i)),
            pl.BlockSpec((share, tile), lambda i: (0, i)),
        ],
        out_shape=[
            jax.ShapeDtypeStruct((depth, vocab), F32),
            jax.ShapeDtypeStruct((share, vocab), BF16),
        ],
        scratch_shapes=[
            pltpu.VMEM((vocab, rows), BF16),
            pltpu.VMEM((depth, rows), BF16),
            pltpu.SemaphoreType.DMA((len(blocks),)),
            pltpu.SemaphoreType.DMA,
        ],
        compiler_params=params(58),
        cost_estimate=pl.CostEstimate(
            flops=2 * rows * depth * vocab, bytes_accessed=12 * MIB, transcendentals=0
        ),
    )(where, *blocks, features)


def ring_shift(values, step, size):
    return lax.ppermute(values, RING, [(i, (i + step) % size) for i in range(size)])


def ring_gather(halves, size):
    blocks, hops = list(halves), [(0, 0), (0, 1)]
    ahead, behind = list(halves), list(halves)
    for step in range(1, size // 2 + 1):
        last = step == size // 2
        for half in range(2):
            if not last or half == 1:
                ahead[half] = ring_shift(ahead[half], 1, size)
                blocks.append(ahead[half])
                hops.append((step, half))
            if not last or half == 0:
                behind[half] = ring_shift(behind[half], -1, size)
                blocks.append(behind[half])
                hops.append((size - step, half))
    return blocks, hops


def to_all(values, axis, **groups):
    size = lax.axis_size(axis)
    if groups:
        size = len(groups["axis_index_groups"][0])
    return lax.all_to_all(jnp.broadcast_to(values[None], (size,) + values.shape), axis, 0, 0, **groups)


def spread(column, chips_x, chips_y):
    def shift(values, x, y, core):
        pairs = []
        for i in range(chips_x):
            for j in range(chips_y):
                for c in range(2):
                    target = ((i + x) % chips_x * chips_y + (j + y) % chips_y) * 2 + (c ^ core)
                    pairs.append(((i * chips_y + j) * 2 + c, target))
        return lax.ppermute(values, "voc", pairs)

    half = column.shape[1] // 2
    first, second = column[:, :half], column[:, half:]
    along_x = [first] + [shift(first, k, 0, 0) for k in range(1, chips_x)]
    along_y = [second] + [shift(second, 0, k, 0) for k in range(1, chips_y)]
    along_x, along_y = lax.optimization_barrier((along_x, along_y))
    first, second = jnp.concatenate(along_x), jnp.concatenate(along_y)
    arrays = [(first, [(i, 0) for i in range(chips_x)], 0), (second, [(0, i) for i in range(chips_y)], 1)]
    for k in range(1, max(chips_x, chips_y)):
        if k < chips_y:
            arrays.append((shift(first, 0, k, 0), [(i, k) for i in range(chips_x)], 0))
        if k < chips_x:
            arrays.append((shift(second, k, 0, 0), [(k, i) for i in range(chips_y)], 1))
    values = lax.optimization_barrier([array for array, _, _ in arrays])
    out, origins = [], []
    for (_, steps, which), value in zip(arrays, values):
        out += [value, shift(value, 0, 0, 1)]
        origins += [(steps, 0, which), (steps, 1, which)]
    return out, origins


def on_device(hidden, head, pool, lines, sizes):
    toks, subs, vocs = lax.axis_size("tok"), lax.axis_size("sub"), lax.axis_size("voc")
    ring = toks * subs
    chips = vocs // 2
    share, width = hidden.shape
    rows = share * ring
    depth, vocab = head.shape
    cut = vocab // ring
    kept = lines.shape[0]
    tok = lax.axis_index("tok")
    place = lax.axis_index(RING)
    voc = lax.axis_index("voc")
    where = jnp.stack([place, voc % 2, voc, tok])
    cores = [(i, i ^ 1) for i in range(vocs)]
    groups = [[2 * i + c for i in range(chips)] for c in range(2)]

    wanted = lines - tok * pool.shape[0]
    choose = (
        lax.broadcasted_iota(jnp.int32, (pool.shape[0], kept), 0) == wanted[None, :]
    ).astype(BF16)
    picked = lax.dot_general(
        pool, choose, (((0,), (0,)), ((), ())), preferred_element_type=F32
    ).astype(BF16).reshape(toks, cut, kept)
    parts = []
    for shift in range(toks):
        part = lax.dynamic_index_in_dim(picked, (tok + shift) % toks, 0, keepdims=False)
        if shift:
            part = lax.ppermute(part, "tok", [(i, (i + shift) % toks) for i in range(toks)])
        parts.append(part)

    piece = width // vocs
    own = lax.dynamic_slice_in_dim(hidden, voc * piece, piece, 1)
    column = to_all(own, RING)
    slices = head.T.reshape(ring, cut, depth)
    teachers = stack_teachers(where, parts)
    slices, column, teachers = lax.optimization_barrier((slices, column, teachers))
    side = math.isqrt(chips)
    arrays, origins = spread(column.reshape(rows, piece).T, side, side)
    features = assemble(where, arrays, origins, side)
    head_cut = lax.all_to_all(slices, ("sub", "tok"), 0, 0)
    weights = row_weights(sizes, rows).reshape(rows // 128, 128)

    student, stats = student_logits(head_cut, features, teachers, subs)
    mixed = [
        [(t * vocs + 2 * i + c) * subs + u for t in range(toks) for c in range(2) for u in range(subs)]
        for i in range(chips)
    ]
    stats = merge(lax.all_to_all(stats, ("tok", "voc", "sub"), 0, 0, axis_index_groups=mixed))
    stats = jnp.broadcast_to(stats[None], (chips,) + stats.shape)
    stats = lax.all_to_all(stats, "voc", 0, 0, axis_index_groups=groups)
    low, high, divergence = logit_grads(where, stats, weights, student, teachers)
    blocks, hops = ring_gather((low, high), ring)

    part = early_features(where, blocks[:-2], hops[:-2], head)
    keep, give = late_features(where, blocks[-2:], hops[-2:], head, part, ring, rows // vocs)
    given = lax.ppermute(give, "voc", cores)
    sums, where = lax.optimization_barrier(((keep + given.astype(F32)).astype(BF16), where))
    sums = lax.all_to_all(sums, "voc", 0, 0, axis_index_groups=groups)
    feature_grad = jnp.sum(sums.astype(F32), axis=0)

    head_grad, local_grad = head_parts(where, blocks, hops, features, depth, vocab, share)
    return head_grad, feature_grad, local_grad, divergence.reshape(share)


def solution(mesh):
    return jax.shard_map(
        on_device,
        mesh=mesh,
        in_specs=(
            P(RING, None),
            P(RING, "voc"),
            P("tok", ("voc", "sub")),
            P("tok"),
            P(),
        ),
        out_specs=(
            P(RING, "voc"),
            P("voc", RING),
            P(RING, "voc"),
            P(RING),
        ),
        check_vma=False,
    )
```
